32 devices in a mesh: batch: 8 (over z, x), mp: 4 (over y, core).
Axes of the slice: x: 2, y: 2, z: 4, core: 2. Of those that a mesh axis runs over, the one named last changes fastest.
Arguments:
- tokens: bfloat16 [8, 256, 2048], P('batch'), may hold values from -6 to 6
- patches: bfloat16 [8, 256, 1664], P('batch'), may hold values from -6 to 6
- lengths: int32 [8], P('batch'), may hold values from 1 to 256, as said below
- patch_keep: int32 [8, 256], P('batch'), may hold values from 0 to 1, as said below
- norm_gains: bfloat16 [3, 2048], P(None, 'batch'), may hold values from 0.5 to 1.5
- self_qkv: bfloat16 [3, 2048, 2048], P(None, 'batch', 'mp'), may hold values from -0.125 to 0.125
- self_out: bfloat16 [2048, 2048], P('mp', 'batch'), may hold values from -0.5 to 0.5
- cross_q: bfloat16 [2048, 2048], P('batch', 'mp'), may hold values from -0.125 to 0.125
- cross_kv: bfloat16 [2, 2048, 2048], P(None, 'batch', 'mp'), may hold values from -0.125 to 0.125
- cross_out: bfloat16 [2048, 2048], P('mp', 'batch'), may hold values from -1 to 1
- patch_proj: bfloat16 [1664, 2048], P('batch', 'mp'), may hold values from -0.15625 to 0.15625
- ffn_in: bfloat16 [2, 2048, 5120], P(None, 'batch', 'mp'), may hold values from -0.125 to 0.125
- ffn_out: bfloat16 [5120, 2048], P('mp', 'batch'), may hold values from -0.125 to 0.125
- cotangent: bfloat16 [8, 256, 2048], P('batch'), may hold values from -6 to 6
Outputs:
- output: bfloat16 [8, 256, 2048], P('batch')
- input_grad: float32 [8, 256, 2048], P('batch')
- gains_grad: float32 [3, 2048], P(None, 'batch')
- self_qkv_grad: float32 [3, 2048, 2048], P(None, 'batch', 'mp')
- self_out_grad: float32 [2048, 2048], P('mp', 'batch')
- cross_q_grad: float32 [2048, 2048], P('batch', 'mp')
- cross_kv_grad: float32 [2, 2048, 2048], P(None, 'batch', 'mp')
- cross_out_grad: float32 [2048, 2048], P('mp', 'batch')
- patch_proj_grad: float32 [1664, 2048], P('batch', 'mp')
- ffn_in_grad: float32 [2, 2048, 5120], P(None, 'batch', 'mp')
- ffn_out_grad: float32 [5120, 2048], P('mp', 'batch')
The draws below stay inside these ranges and needn't reach their ends.
Inputs may be any that keep to these rules, and one draw needn't show every extreme that they name: `lengths`: slots at or beyond an item's length are padding; some item has length 256. `patch_keep`: 1 marks a patch token that may be attended to; the first patch token of every item is 1.
All inputs are finite; a program needn't handle non-finite values.
Results may differ from the reference program's by a relative error of at most 0.03.
Values may be sent and summed in bfloat16 or wider, within the bound.
A program may use at most 320 MiB of HBM per device.

```python
import jax
import jax.numpy as jnp
from jax import lax

D = 2048
HEADS = 32
HD = 64
FF = 5120
PD = 1664
TEXT = 256
PATCH = 256
ITEMS_DEV = 1
ITEMS = 8
N_MP = 4


def draw_lengths(key, part):
    key = jax.random.fold_in(key, 11)
    first_key, second_key = jax.random.split(key)
    base = jax.random.randint(first_key, (ITEMS,), 1, TEXT + 1)
    spread = base * base // TEXT * base // TEXT
    chosen = jax.random.randint(second_key, (), 0, ITEMS)
    spread = jnp.where(jnp.arange(ITEMS) == chosen, TEXT, spread)
    return jnp.maximum(spread, 1).astype(jnp.int32)


def draw_patch_keep(key, part):
    key = jax.random.fold_in(key, 23)
    picks = jax.random.randint(key, (ITEMS, PATCH), 0, 8)
    kept = (picks > 0).astype(jnp.int32)
    return kept.at[:, 0].set(1)


def block_levels(stream_key, shape, pieces, least, top_value):
    def one(axis_at, blocks):
        heights = jax.random.uniform(jax.random.fold_in(jax.random.fold_in(stream_key, 6), axis_at), (blocks,), jnp.float32, least / len(pieces), top_value / len(pieces))
        return jnp.repeat(jnp.exp(heights), shape[axis_at] // blocks).reshape((-1,) + (1,) * (len(shape) - axis_at - 1))

    factor_of = one(*pieces[0])
    for cut in pieces[1:]:
        factor_of = factor_of * one(*cut)
    return factor_of


def scatter_about(key, extent, scale, bound, cuts=(), held_as=jnp.bfloat16):
    entries = scale * jax.random.normal(key, extent, jnp.float32)
    if cuts:
        entries = entries * block_levels(key, extent, cuts, -0.22, 0.18)
    return jnp.clip(entries, -bound, bound).astype(held_as)


def setup_inputs(seed: int = 0) -> dict:
    key_list = jax.random.split(jax.random.key(seed), 15)
    tokens = scatter_about(key_list[0], (ITEMS, TEXT, D), 1.0, 6.0, ((0, 8),))
    patches = scatter_about(key_list[1], (ITEMS, PATCH, PD), 1.0, 6.0, ((0, 8),))
    lengths = draw_lengths(jax.random.fold_in(key_list[14], 71), 0)
    patch_keep = draw_patch_keep(jax.random.fold_in(key_list[14], 71), 0)
    norm_gains = jnp.clip(1.0 + 0.1 * jax.random.normal(key_list[4], (3, D), jnp.float32), 0.5, 1.5).astype(jnp.bfloat16)
    self_qkv = scatter_about(key_list[5], (3, D, HEADS * HD), D ** -0.5, 0.125, ((1, 8), (2, 4)))
    self_out = scatter_about(key_list[6], (HEADS * HD, D), (HEADS * HD // 16) ** -0.5, 0.5, ((0, 4), (1, 8)))
    cross_q = scatter_about(key_list[7], (D, HEADS * HD), D ** -0.5, 0.125, ((0, 8), (1, 4)))
    cross_kv = scatter_about(key_list[8], (2, D, HEADS * HD), D ** -0.5, 0.125, ((1, 8), (2, 4)))
    cross_out = scatter_about(key_list[9], (HEADS * HD, D), (HEADS * HD // 64) ** -0.5, 1.0, ((0, 4), (1, 8)))
    patch_proj = scatter_about(key_list[10], (PD, D), PD ** -0.5, 0.15625, ((0, 8), (1, 4)))
    ffn_in = scatter_about(key_list[11], (2, D, FF), D ** -0.5, 0.125, ((1, 8), (2, 4)))
    ffn_out = scatter_about(key_list[12], (FF, D), (FF // 2) ** -0.5, 0.125, ((0, 4), (1, 8)))
    cotangent = scatter_about(key_list[13], (ITEMS, TEXT, D), 1.0, 6.0, ((0, 8),))
    return {"tokens": tokens, "patches": patches, "lengths": lengths, "patch_keep": patch_keep, "norm_gains": norm_gains, "self_qkv": self_qkv, "self_out": self_out, "cross_q": cross_q, "cross_kv": cross_kv, "cross_out": cross_out, "patch_proj": patch_proj, "ffn_in": ffn_in, "ffn_out": ffn_out, "cotangent": cotangent}


@jax.custom_vjp
def low(v):
    return lax.optimization_barrier(v.astype(jnp.bfloat16)).astype(jnp.float32)

@jax.custom_vjp
def low_back(v):
    return v

def low_keep(v):
    return (low(v), None)

def low_pass(kept, grad):
    return (grad,)

def back_keep(v):
    return (v, None)

def back_low(kept, grad):
    return (low(grad),)
low.defvjp(low_keep, low_pass)
low_back.defvjp(back_keep, back_low)
epsilon = 1e-06
highest = lax.Precision.HIGHEST

def rms_scale(values, gain):
    return values * lax.rsqrt(lax.optimization_barrier(jnp.mean(values * values, axis=-1, keepdims=True)) + epsilon) * gain

def split_heads(values):
    return values.reshape(values.shape[0], values.shape[1], HEADS, HD)

def attend(queries, key_rows, value_rows, allowed):
    scores = low_back(jnp.einsum('bshe,bkhe->bhsk', queries, key_rows, precision=highest) * HD ** (-0.5))
    scores = jnp.where(allowed[:, None], scores, -1000000000.0)
    attn_probs = jax.nn.softmax(scores, axis=-1)
    mixed = jnp.einsum('bhsk,bkhe->bshe', low(attn_probs), value_rows, precision=highest)
    return low(low_back(mixed.reshape(mixed.shape[0], mixed.shape[1], HEADS * HD)))

def branch_sum(mixed, weight):
    grouped = mixed.reshape(mixed.shape[0], mixed.shape[1], N_MP, -1)
    blocks = weight.reshape(N_MP, -1, D)
    partial_value = jnp.einsum('bsgk,gkd->bsgd', grouped, blocks, precision=highest)
    return low_back(lax.optimization_barrier(jnp.sum(low(partial_value), axis=2)))

def layer_block(inputs, sources, lengths, patch_keep, weights):
    norm_gains, self_qkv, self_out, cross_q, cross_kv, cross_out, patch_proj, ffn_in, ffn_out = weights
    slot_count = inputs.shape[1]
    row_index = lax.broadcasted_iota(jnp.int32, (slot_count, slot_count), 0)
    col_index = lax.broadcasted_iota(jnp.int32, (slot_count, slot_count), 1)
    self_allowed = (col_index <= row_index)[None] & (col_index[None] < lengths[:, None, None])
    normed = low(rms_scale(inputs, norm_gains[0]))
    projected = low(low_back(jnp.einsum('bsd,cdf->cbsf', normed, self_qkv, precision=highest)))
    mixed = attend(split_heads(projected[0]), split_heads(projected[1]), split_heads(projected[2]), self_allowed)
    after_self = inputs + branch_sum(mixed, self_out)
    normed = low(rms_scale(after_self, norm_gains[1]))
    queries = low(low_back(jnp.einsum('bsd,df->bsf', normed, cross_q, precision=highest)))
    memory = low(low_back(jnp.einsum('bpk,kd->bpd', sources, patch_proj, precision=highest)))
    key_value = low(low_back(jnp.einsum('bpd,cdf->cbpf', memory, cross_kv, precision=highest)))
    cross_allowed = (patch_keep > 0)[:, None, :]
    mixed = attend(split_heads(queries), split_heads(key_value[0]), split_heads(key_value[1]), cross_allowed)
    after_cross = after_self + branch_sum(mixed, cross_out)
    normed = low(rms_scale(after_cross, norm_gains[2]))
    gate_up = low_back(jnp.einsum('bsd,cdf->cbsf', normed, ffn_in, precision=highest))
    hidden = low(jax.nn.gelu(gate_up[0], approximate=True) * gate_up[1])
    return after_cross + branch_sum(hidden, ffn_out)

def reference(tokens, patches, lengths, patch_keep, norm_gains, self_qkv, self_out, cross_q, cross_kv, cross_out, patch_proj, ffn_in, ffn_out, cotangent):
    weights = tuple((matrix.astype(jnp.float32) for matrix in (norm_gains, self_qkv, self_out, cross_q, cross_kv, cross_out, patch_proj, ffn_in, ffn_out)))
    inputs = tokens.astype(jnp.float32)
    sources = patches.astype(jnp.float32).reshape(-1, ITEMS_DEV, PATCH, PD)
    length_groups = lengths.reshape(-1, ITEMS_DEV)
    keep_groups = patch_keep.reshape(-1, ITEMS_DEV, PATCH)

    def forward(layer_in, layer_weights):

        def one_group(group):
            return layer_block(group[0], group[1], group[2], group[3], layer_weights)
        grouped = lax.map(jax.checkpoint(one_group), (layer_in.reshape(-1, ITEMS_DEV, TEXT, D), sources, length_groups, keep_groups))
        return grouped.reshape(ITEMS, TEXT, D)
    output, pullback = jax.vjp(forward, inputs, weights)
    grad_inputs, grad_weights = pullback(cotangent.astype(jnp.float32))
    return (output.astype(jnp.bfloat16), grad_inputs, grad_weights[0], grad_weights[1], grad_weights[2], grad_weights[3], grad_weights[4], grad_weights[5], grad_weights[6], grad_weights[7], grad_weights[8])
```

```python
import functools

import jax
import jax.numpy as jnp
from jax import lax
from jax.experimental import pallas as pl
from jax.experimental.pallas import tpu as pltpu
from jax.sharding import Mesh
from jax.sharding import PartitionSpec as P

HD = 64
EPS = 1e-06
RELATIVE = ((1, 1), (1, 0), (0, 1), (0, 0))
VMEM_LIMIT = 48 * 2**20


def rounded(values):
    return values.astype(jnp.bfloat16)


def flip(value, by):
    return value + by * (1 - 2 * value)


class Plane:
    def __init__(self):
        self.x = lax.axis_index("x")
        part = lax.axis_index("mp")
        self.y = part // 2
        self.c = part % 2

    def device(self, dx, dy, dc):
        return {"x": flip(self.x, dx), "mp": flip(self.y, dy) * 2 + flip(self.c, dc)}

    def block(self, dx, dy, dc):
        return (flip(self.x, dx) * 2 + flip(self.y, dy)) * 2 + flip(self.c, dc)

    def greet(self, relations):
        barrier = pltpu.get_barrier_semaphore()
        for relation in relations:
            pl.semaphore_signal(
                barrier, inc=1, device_id=self.device(*relation), device_id_type=pl.DeviceIdType.MESH
            )
        pl.semaphore_wait(barrier, len(relations))

    def send(self, src, dst, sems, slot, relation):
        copy = pltpu.make_async_remote_copy(
            src_ref=src,
            dst_ref=dst,
            send_sem=sems.at[0, slot],
            recv_sem=sems.at[1, slot],
            device_id=self.device(*relation),
            device_id_type=pl.DeviceIdType.MESH,
        )
        copy.start()
        return copy


ALL_RELATIONS = ((0, 0, 1), (1, 1, 0), (1, 0, 0), (0, 1, 0))
ROW_RELATIONS = ((0, 0, 1), (0, 1, 0))


def reduce_blocks(plane, part, from_core, to_chip, from_chip, sems):
    pair = [
        plane.send(part.at[plane.block(dx, dy, 1)], from_core.at[i], sems, i, (0, 0, 1))
        for i, (dx, dy) in enumerate(RELATIVE)
    ]
    across = []
    for i, (dx, dy) in enumerate(RELATIVE):
        pair[i].wait_recv()
        both = part[plane.block(dx, dy, 0)].astype(jnp.float32) + from_core[i].astype(jnp.float32)
        if i < 3:
            to_chip[i] = rounded(both)
            across.append(plane.send(to_chip.at[i], from_chip.at[i], sems, 4 + i, (dx, dy, 0)))
    for i in (2, 1, 0):
        across[i].wait_recv()
        both = both + from_chip[i].astype(jnp.float32)
    for copy in pair + across:
        copy.wait_send()
    return both


def gather_blocks(plane, out, sems, first):
    mine = plane.block(0, 0, 0)
    sends = [
        plane.send(out.at[mine], out.at[mine], sems, first + i, (dx, dy, 0))
        for i, (dx, dy) in enumerate(RELATIVE[:3])
    ]
    sends.append(plane.send(out.at[mine], out.at[mine], sems, first + 3, (0, 0, 1)))
    for i in (2, 1, 0):
        dx, dy = RELATIVE[i]
        theirs = plane.block(dx, dy, 0)
        sends[i].wait_recv()
        sends.append(plane.send(out.at[theirs], out.at[theirs], sems, first + 4 + i, (0, 0, 1)))
    for copy in sends[3:]:
        copy.wait_recv()
    for copy in sends:
        copy.wait_send()


def gather_rows(plane, out, sems, first):
    mine = plane.y * 2 + plane.c
    theirs = flip(plane.y, 1) * 2 + plane.c
    over = plane.send(out.at[mine], out.at[mine], sems, first, (0, 1, 0))
    beside = plane.send(out.at[mine], out.at[mine], sems, first + 1, (0, 0, 1))
    over.wait_recv()
    onward = plane.send(out.at[theirs], out.at[theirs], sems, first + 2, (0, 0, 1))
    beside.wait_recv()
    onward.wait_recv()
    for copy in (over, beside, onward):
        copy.wait_send()


def forward_kernel(part, residual, gain, after, normed, from_core, to_chip, from_chip, sems):
    plane = Plane()
    plane.greet(ALL_RELATIONS)
    values = residual[...] + reduce_blocks(plane, part, from_core, to_chip, from_chip, sems)
    after[...] = values
    scale = lax.rsqrt(jnp.mean(values * values, axis=-1, keepdims=True) + EPS)
    normed[plane.block(0, 0, 0)] = rounded(values * scale * gain[...])
    gather_blocks(plane, normed, sems, 7)


def back_values(values, gain, grad):
    scale = lax.rsqrt(jnp.mean(values * values, axis=-1, keepdims=True) + EPS)
    gain_part = jnp.sum(grad * values * scale, axis=0, keepdims=True)
    scaled = grad * gain
    side = scale * scaled - values * (scale * scale * scale) * jnp.mean(
        scaled * values, axis=-1, keepdims=True
    )
    return side, gain_part


def backward_kernel(
    part, values, grad, gain, grad_out, gain_part, grad_all, from_core, to_chip, from_chip, sems
):
    plane = Plane()
    plane.greet(ALL_RELATIONS)
    total = reduce_blocks(plane, part, from_core, to_chip, from_chip, sems)
    side, gain_sum = back_values(values[...], gain[...], total)
    gain_part[...] = gain_sum
    result = grad[...] + side
    grad_out[...] = result
    grad_all[plane.block(0, 0, 0)] = rounded(result)
    gather_blocks(plane, grad_all, sems, 7)


def output_kernel(part, residual, out, from_core, to_chip, from_chip, sems):
    plane = Plane()
    plane.greet(ALL_RELATIONS)
    values = residual[...] + reduce_blocks(plane, part, from_core, to_chip, from_chip, sems)
    out[plane.y * 2 + plane.c] = rounded(values)
    gather_rows(plane, out, sems, 7)


def input_kernel(part, values, grad, gain, out, gain_part, from_core, to_chip, from_chip, sems):
    plane = Plane()
    plane.greet(ALL_RELATIONS)
    total = reduce_blocks(plane, part, from_core, to_chip, from_chip, sems)
    side, gain_sum = back_values(values[...], gain[...], total)
    gain_part[...] = gain_sum
    out[plane.y * 2 + plane.c] = grad[...] + side
    gather_rows(plane, out, sems, 7)


def gather_kernel(own, out, sems):
    plane = Plane()
    plane.greet(ALL_RELATIONS)
    out[plane.block(0, 0, 0)] = own[...]
    gather_blocks(plane, out, sems, 0)


def scatter_kernel(part, out, from_core, to_chip, from_chip, sems):
    plane = Plane()
    plane.greet(ALL_RELATIONS)
    out[...] = rounded(reduce_blocks(plane, part, from_core, to_chip, from_chip, sems))


def plane_call(kernel, name, number, outs, rows, columns, copies, reduces, operands):
    whole = pl.BlockSpec(memory_space=pltpu.VMEM)
    scratch = []
    if reduces:
        scratch = [
            pltpu.VMEM((4, rows, columns), jnp.bfloat16),
            pltpu.VMEM((3, rows, columns), jnp.bfloat16),
            pltpu.VMEM((3, rows, columns), jnp.bfloat16),
        ]
    scratch.append(pltpu.SemaphoreType.DMA((2, copies)))
    return pl.pallas_call(
        kernel,
        name=name,
        out_shape=outs,
        in_specs=[whole] * len(operands),
        out_specs=jax.tree.map(lambda _: whole, outs),
        scratch_shapes=scratch,
        compiler_params=pltpu.CompilerParams(
            collective_id=number, has_side_effects=True, vmem_limit_bytes=VMEM_LIMIT
        ),
    )(*operands)


def full(shape, dtype=jnp.float32):
    return jax.ShapeDtypeStruct(shape, dtype)


def forward_step(part, residual, gain):
    rows, columns = residual.shape
    return plane_call(
        forward_kernel, "forward_step", 0,
        (full((rows, columns)), full((8, rows, columns), jnp.bfloat16)),
        rows, columns, 14, True, (part, residual, gain),
    )


def backward_step(part, values, grad, gain):
    rows, columns = values.shape
    return plane_call(
        backward_kernel, "backward_step", 1,
        (full((rows, columns)), full((1, columns)), full((8, rows, columns), jnp.bfloat16)),
        rows, columns, 14, True, (part, values, grad, gain),
    )


def output_step(part, residual):
    rows, columns = residual.shape
    return plane_call(
        output_kernel, "output_step", 2, full((4, rows, columns), jnp.bfloat16),
        rows, columns, 10, True, (part, residual),
    )


def input_step(part, values, grad, gain):
    rows, columns = values.shape
    return plane_call(
        input_kernel, "input_step", 3, (full((4, rows, columns)), full((1, columns))),
        rows, columns, 10, True, (part, values, grad, gain),
    )


def gather_step(own):
    rows, columns = own.shape
    return plane_call(
        gather_kernel, "gather_step", 4, full((8, rows, columns), own.dtype),
        rows, columns, 7, False, (own,),
    )


def scatter_step(part):
    _, rows, columns = part.shape
    return plane_call(
        scatter_kernel, "scatter_step", 5, full((rows, columns), part.dtype),
        rows, columns, 7, True, (part,),
    )


def split_heads(values):
    return values.reshape(2, values.shape[0] // 2, -1, HD)


def merge_heads(values):
    return values.reshape(2 * values.shape[1], -1)


def masked_scores(queries, key_rows, allowed):
    scores = jnp.einsum(
        "bshe,bkhe->bhsk", queries, key_rows, preferred_element_type=jnp.float32
    ) * HD ** (-0.5)
    return jnp.where(allowed[:, None], scores, -1000000000.0)


def attend(queries, key_rows, value_rows, allowed):
    scores = masked_scores(queries, key_rows, allowed)
    log_total = jax.nn.logsumexp(scores, axis=-1, keepdims=True)
    attn_probs = jnp.exp(scores - log_total)
    mixed = jnp.einsum(
        "bhsk,bkhe->bshe", rounded(attn_probs), value_rows, preferred_element_type=jnp.float32
    )
    return (rounded(merge_heads(mixed)), log_total)


def attend_back(queries, key_rows, value_rows, allowed, log_total, grad_mixed):
    attn_probs = jnp.exp(masked_scores(queries, key_rows, allowed) - log_total)
    grad_probs = jnp.einsum(
        "bshe,bkhe->bhsk", grad_mixed, value_rows, preferred_element_type=jnp.float32
    )
    grad_scores = rounded(
        attn_probs * (grad_probs - jnp.sum(attn_probs * grad_probs, axis=-1, keepdims=True))
    )
    grad_queries = jnp.einsum(
        "bhsk,bkhe->bshe", grad_scores, key_rows, preferred_element_type=jnp.float32
    ) * HD ** (-0.5)
    grad_keys = jnp.einsum(
        "bhsk,bshe->bkhe", grad_scores, queries, preferred_element_type=jnp.float32
    ) * HD ** (-0.5)
    grad_values = jnp.einsum(
        "bhsk,bshe->bkhe", rounded(attn_probs), grad_mixed, preferred_element_type=jnp.float32
    )
    return tuple(rounded(merge_heads(g)) for g in (grad_queries, grad_keys, grad_values))


def gated_gelu(gate_up):
    return jax.nn.gelu(gate_up[0], approximate=True) * gate_up[1]


def dot(pattern, left, right):
    return jnp.einsum(pattern, left, right, preferred_element_type=jnp.float32)


SWAP = ((0, 1), (1, 0))


def halves(values, axis, x):
    size = values.shape[axis] // 2
    keep = lax.dynamic_slice_in_dim(values, x * size, size, axis)
    give = lax.dynamic_slice_in_dim(values, (1 - x) * size, size, axis)
    return keep, give


def in_order(own, other, axis, x):
    return jnp.where(
        x == 0,
        jnp.concatenate([own, other], axis),
        jnp.concatenate([other, own], axis),
    )


def exchange(values, cut, join, x):
    keep, give = halves(values, cut, x)
    return in_order(keep, lax.ppermute(give, "x", SWAP), join, x)


def both_items(values, x):
    return in_order(values, lax.ppermute(values, "x", SWAP), 0, x)


def gather_in(weight, x):
    swapped = exchange(weight, weight.ndim - 1, weight.ndim - 2, x)
    return lax.all_gather(swapped, "z", axis=weight.ndim - 2, tiled=True)


def gather_out(weight, x):
    return lax.all_gather(exchange(weight, 0, 1, x), "z", axis=0, tiled=False)


def scatter_in(grad, x):
    share = lax.psum_scatter(rounded(grad), "z", scatter_dimension=grad.ndim - 2, tiled=True)
    return exchange(share, grad.ndim - 2, grad.ndim - 1, x).astype(jnp.float32)


def scatter_out(grad, x):
    share = lax.psum_scatter(rounded(grad), "z", scatter_dimension=0, tiled=False)
    return exchange(share, 1, 0, x).astype(jnp.float32)


def on_device(
    tokens,
    patches,
    lengths,
    patch_keep,
    norm_gains,
    self_qkv,
    self_out,
    cross_q,
    cross_kv,
    cross_out,
    patch_proj,
    ffn_in,
    ffn_out,
    cotangent,
):
    x = lax.axis_index("x")
    m = lax.axis_index("mp")
    slots, width = tokens.shape[1], tokens.shape[2]
    rows = slots // 4
    gains = lax.all_gather(norm_gains, ("z", "x"), axis=1, tiled=True).astype(jnp.float32)
    gain_of = [gains[i : i + 1] for i in range(3)]
    facts = jnp.concatenate([patch_keep, lengths[:, None]], axis=1)
    facts = lax.all_gather(facts, "x", axis=0, tiled=True)
    patch_keep, lengths = facts[:, :-1], facts[:, -1]

    patch_w = gather_in(patch_proj, x)
    qkv_w = gather_in(self_qkv, x)
    self_out_w = gather_out(self_out, x)
    cross_kv_w = gather_in(cross_kv, x)
    cross_q_w = gather_in(cross_q, x)
    cross_out_w = gather_out(cross_out, x)
    ffn_in_w = gather_in(ffn_in, x)
    ffn_out_w = gather_out(ffn_out, x)

    row_index = lax.broadcasted_iota(jnp.int32, (slots, slots), 0)
    col_index = lax.broadcasted_iota(jnp.int32, (slots, slots), 1)
    self_allowed = (col_index <= row_index)[None] & (col_index[None] < lengths[:, None, None])
    cross_allowed = (patch_keep > 0)[:, None, :]

    token_all = both_items(tokens[0], x)
    patch_all = both_items(patches[0], x)
    grad_all = both_items(cotangent[0], x)
    own_tokens = lax.dynamic_slice_in_dim(tokens[0], m * rows, rows, 0).astype(jnp.float32)
    own_grad = lax.dynamic_slice_in_dim(cotangent[0], m * rows, rows, 0).astype(jnp.float32)

    values = token_all.astype(jnp.float32)
    normed_self = rounded(
        values
        * lax.rsqrt(jnp.mean(values * values, axis=-1, keepdims=True) + EPS)
        * gain_of[0]
    )

    def to_blocks(partial_value):
        return rounded(partial_value).reshape(8, rows, width)

    def from_blocks(blocks):
        return blocks.reshape(8 * rows, width)

    memory_part = rounded(dot("pk,kd->pd", patch_all, patch_w))
    memory_blocks = gather_step(memory_part)
    memory = (
        memory_blocks.reshape(2, 4, memory_part.shape[0], -1)
        .transpose(2, 1, 0, 3)
        .reshape(memory_part.shape[0], -1)
    )

    projected = rounded(dot("sd,cdf->csf", normed_self, qkv_w))
    self_parts = [split_heads(projected[i]) for i in range(3)]
    mixed_self, total_self = attend(*self_parts, self_allowed)
    part = dot("sk,zkd->szd", mixed_self, self_out_w)
    after_self, normed_cross = forward_step(to_blocks(part), own_tokens, gain_of[1])
    normed_cross = from_blocks(normed_cross)

    key_value = rounded(dot("pd,cdf->cpf", memory, cross_kv_w))
    query_heads = split_heads(rounded(dot("sd,df->sf", normed_cross, cross_q_w)))
    cross_keys = split_heads(key_value[0])
    cross_values = split_heads(key_value[1])
    mixed_cross, total_cross = attend(query_heads, cross_keys, cross_values, cross_allowed)
    part = dot("sk,zkd->szd", mixed_cross, cross_out_w)
    after_cross, normed_ffn = forward_step(to_blocks(part), after_self, gain_of[2])
    normed_ffn = from_blocks(normed_ffn)

    gate_up = dot("sd,cdf->csf", normed_ffn, ffn_in_w)
    hidden = rounded(gated_gelu(gate_up))
    part = dot("sf,zfd->szd", hidden, ffn_out_w)
    output = output_step(to_blocks(part), after_cross).reshape(1, slots, width)

    cuts = ffn_out_w.shape[0]

    def cut(grad):
        return grad.reshape(grad.shape[0], cuts, -1)

    grad_ffn_out = scatter_out(dot("sf,szd->zfd", hidden, cut(grad_all)), x)
    grad_hidden = dot("szd,zfd->sf", cut(grad_all), ffn_out_w)
    grad_gate_up = rounded(jax.vjp(gated_gelu, gate_up)[1](grad_hidden)[0])
    grad_ffn_in = scatter_in(dot("sd,csf->cdf", normed_ffn, grad_gate_up), x)
    part = dot("csf,cdf->sd", grad_gate_up, ffn_in_w)
    grad_after_cross, gain_ffn, grad_all = backward_step(
        to_blocks(part), after_cross, own_grad, gain_of[2]
    )
    grad_all = from_blocks(grad_all)

    grad_cross_out = scatter_out(dot("sk,szd->zkd", mixed_cross, cut(grad_all)), x)
    grad_mixed = split_heads(rounded(dot("szd,zkd->sk", cut(grad_all), cross_out_w)))
    grad_queries, grad_keys, grad_values = attend_back(
        query_heads, cross_keys, cross_values, cross_allowed, total_cross, grad_mixed
    )
    part = dot("sf,df->sd", grad_queries, cross_q_w)
    grad_after_self, gain_cross, grad_all = backward_step(
        to_blocks(part), after_self, grad_after_cross, gain_of[1]
    )
    grad_all = from_blocks(grad_all)
    grad_key_value = jnp.stack([grad_keys, grad_values])
    grad_cross_q = scatter_in(dot("sd,sf->df", normed_cross, grad_queries), x)
    grad_cross_kv = scatter_in(dot("pd,cpf->cdf", memory, grad_key_value), x)
    part = rounded(dot("cpf,cdf->pd", grad_key_value, cross_kv_w))
    part = part.reshape(part.shape[0], 4, 2, -1).transpose(2, 1, 0, 3)
    grad_memory = scatter_step(part.reshape(8, *memory_part.shape))
    grad_patch = scatter_in(dot("pk,pd->kd", patch_all, grad_memory), x)

    grad_self_out = scatter_out(dot("sk,szd->zkd", mixed_self, cut(grad_all)), x)
    grad_mixed = split_heads(rounded(dot("szd,zkd->sk", cut(grad_all), self_out_w)))
    grad_projected = jnp.stack(attend_back(*self_parts, self_allowed, total_self, grad_mixed))
    grad_self_qkv = scatter_in(dot("sd,csf->cdf", normed_self, grad_projected), x)
    part = dot("csf,cdf->sd", grad_projected, qkv_w)
    grad_input, gain_self = input_step(to_blocks(part), own_tokens, grad_after_self, gain_of[0])
    grad_input = grad_input.reshape(1, slots, width)
    grad_gains = jnp.concatenate([gain_self, gain_cross, gain_ffn], axis=0)
    grad_gains = lax.psum_scatter(
        lax.psum(grad_gains, "mp"), ("z", "x"), scatter_dimension=1, tiled=True
    )
    return (
        output,
        grad_input,
        grad_gains,
        grad_self_qkv,
        grad_self_out,
        grad_cross_q,
        grad_cross_kv,
        grad_cross_out,
        grad_patch,
        grad_ffn_in,
        grad_ffn_out,
    )


def solution(mesh):
    batch, parts = mesh.shape["batch"], mesh.shape["mp"]
    planes = Mesh(mesh.devices.reshape(batch // 2, 2, parts), ("z", "x", "mp"))
    b = ("z", "x")
    weights = (
        P(None, b, "mp"),
        P("mp", b),
        P(b, "mp"),
        P(None, b, "mp"),
        P("mp", b),
        P(b, "mp"),
        P(None, b, "mp"),
        P("mp", b),
    )
    row = P(b, None, None)
    return jax.shard_map(
        on_device,
        mesh=planes,
        in_specs=(row, row, P(b), P(b, None), P(None, b)) + weights + (row,),
        out_specs=(row, row, P(None, b)) + weights,
        check_vma=False,
    )
```

```python
import functools

import jax
import jax.numpy as jnp
from jax import lax
from jax.experimental import pallas as pl
from jax.experimental.pallas import tpu as pltpu
from jax.sharding import Mesh
from jax.sharding import PartitionSpec as P

HD = 64
EPS = 1e-06
RELATIVE = ((1, 1), (1, 0), (0, 1), (0, 0))
VMEM_LIMIT = 48 * 2**20


def rounded(values):
    return values.astype(jnp.bfloat16)


def flip(value, by):
    return value + by * (1 - 2 * value)


class Plane:
    def __init__(self):
        self.x = lax.axis_index("x")
        part = lax.axis_index("mp")
        self.y = part // 2
        self.c = part % 2

    def device(self, dx, dy, dc):
        return {"x": flip(self.x, dx), "mp": flip(self.y, dy) * 2 + flip(self.c, dc)}

    def block(self, dx, dy, dc):
        return (flip(self.x, dx) * 2 + flip(self.y, dy)) * 2 + flip(self.c, dc)

    def greet(self, relations):
        barrier = pltpu.get_barrier_semaphore()
        for relation in relations:
            pl.semaphore_signal(
                barrier, inc=1, device_id=self.device(*relation), device_id_type=pl.DeviceIdType.MESH
            )
        pl.semaphore_wait(barrier, len(relations))

    def send(self, src, dst, sems, slot, relation):
        copy = pltpu.make_async_remote_copy(
            src_ref=src,
            dst_ref=dst,
            send_sem=sems.at[0, slot],
            recv_sem=sems.at[1, slot],
            device_id=self.device(*relation),
            device_id_type=pl.DeviceIdType.MESH,
        )
        copy.start()
        return copy


ALL_RELATIONS = ((0, 0, 1), (1, 1, 0), (1, 0, 0), (0, 1, 0))
ROW_RELATIONS = ((0, 0, 1), (0, 1, 0))


def reduce_blocks(plane, part, from_core, to_chip, from_chip, sems):
    pair = [
        plane.send(part.at[plane.block(dx, dy, 1)], from_core.at[i], sems, i, (0, 0, 1))
        for i, (dx, dy) in enumerate(RELATIVE)
    ]
    across = []
    for i, (dx, dy) in enumerate(RELATIVE):
        pair[i].wait_recv()
        both = part[plane.block(dx, dy, 0)].astype(jnp.float32) + from_core[i].astype(jnp.float32)
        if i < 3:
            to_chip[i] = rounded(both)
            across.append(plane.send(to_chip.at[i], from_chip.at[i], sems, 4 + i, (dx, dy, 0)))
    for i in (2, 1, 0):
        across[i].wait_recv()
        both = both + from_chip[i].astype(jnp.float32)
    for copy in pair + across:
        copy.wait_send()
    return both


def gather_blocks(plane, out, sems, first):
    mine = plane.block(0, 0, 0)
    sends = [
        plane.send(out.at[mine], out.at[mine], sems, first + i, (dx, dy, 0))
        for i, (dx, dy) in enumerate(RELATIVE[:3])
    ]
    sends.append(plane.send(out.at[mine], out.at[mine], sems, first + 3, (0, 0, 1)))
    for i in (2, 1, 0):
        dx, dy = RELATIVE[i]
        theirs = plane.block(dx, dy, 0)
        sends[i].wait_recv()
        sends.append(plane.send(out.at[theirs], out.at[theirs], sems, first + 4 + i, (0, 0, 1)))
    for copy in sends[3:]:
        copy.wait_recv()
    for copy in sends:
        copy.wait_send()


def gather_rows(plane, out, sems, first):
    mine = plane.y * 2 + plane.c
    theirs = flip(plane.y, 1) * 2 + plane.c
    over = plane.send(out.at[mine], out.at[mine], sems, first, (0, 1, 0))
    beside = plane.send(out.at[mine], out.at[mine], sems, first + 1, (0, 0, 1))
    over.wait_recv()
    onward = plane.send(out.at[theirs], out.at[theirs], sems, first + 2, (0, 0, 1))
    beside.wait_recv()
    onward.wait_recv()
    for copy in (over, beside, onward):
        copy.wait_send()


def forward_kernel(part, residual, gain, after, normed, from_core, to_chip, from_chip, sems):
    plane = Plane()
    plane.greet(ALL_RELATIONS)
    values = residual[...] + reduce_blocks(plane, part, from_core, to_chip, from_chip, sems)
    after[...] = values
    scale = lax.rsqrt(jnp.mean(values * values, axis=-1, keepdims=True) + EPS)
    normed[plane.block(0, 0, 0)] = rounded(values * scale * gain[...])
    gather_blocks(plane, normed, sems, 7)


def back_values(values, gain, grad):
    scale = lax.rsqrt(jnp.mean(values * values, axis=-1, keepdims=True) + EPS)
    gain_part = jnp.sum(grad * values * scale, axis=0, keepdims=True)
    scaled = grad * gain
    side = scale * scaled - values * (scale * scale * scale) * jnp.mean(
        scaled * values, axis=-1, keepdims=True
    )
    return side, gain_part


def backward_kernel(
    part, values, grad, gain, grad_out, gain_part, grad_all, from_core, to_chip, from_chip, sems
):
    plane = Plane()
    plane.greet(ALL_RELATIONS)
    total = reduce_blocks(plane, part, from_core, to_chip, from_chip, sems)
    side, gain_sum = back_values(values[...], gain[...], total)
    gain_part[...] = gain_sum
    result = grad[...] + side
    grad_out[...] = result
    grad_all[plane.block(0, 0, 0)] = rounded(result)
    gather_blocks(plane, grad_all, sems, 7)


def output_kernel(part, residual, out, from_core, to_chip, from_chip, sems):
    plane = Plane()
    plane.greet(ALL_RELATIONS)
    values = residual[...] + reduce_blocks(plane, part, from_core, to_chip, from_chip, sems)
    out[plane.y * 2 + plane.c] = rounded(values)
    gather_rows(plane, out, sems, 7)


def input_kernel(part, values, grad, gain, out, gain_part, from_core, to_chip, from_chip, sems):
    plane = Plane()
    plane.greet(ALL_RELATIONS)
    total = reduce_blocks(plane, part, from_core, to_chip, from_chip, sems)
    side, gain_sum = back_values(values[...], gain[...], total)
    gain_part[...] = gain_sum
    out[plane.y * 2 + plane.c] = grad[...] + side
    gather_rows(plane, out, sems, 7)


def gather_kernel(own, out, sems):
    plane = Plane()
    plane.greet(ALL_RELATIONS)
    out[plane.block(0, 0, 0)] = own[...]
    gather_blocks(plane, out, sems, 0)


def scatter_kernel(part, out, from_core, to_chip, from_chip, sems):
    plane = Plane()
    plane.greet(ALL_RELATIONS)
    out[...] = rounded(reduce_blocks(plane, part, from_core, to_chip, from_chip, sems))


def plane_call(kernel, name, number, outs, rows, columns, copies, reduces, operands):
    whole = pl.BlockSpec(memory_space=pltpu.VMEM)
    scratch = []
    if reduces:
        scratch = [
            pltpu.VMEM((4, rows, columns), jnp.bfloat16),
            pltpu.VMEM((3, rows, columns), jnp.bfloat16),
            pltpu.VMEM((3, rows, columns), jnp.bfloat16),
        ]
    scratch.append(pltpu.SemaphoreType.DMA((2, copies)))
    return pl.pallas_call(
        kernel,
        name=name,
        out_shape=outs,
        in_specs=[whole] * len(operands),
        out_specs=jax.tree.map(lambda _: whole, outs),
        scratch_shapes=scratch,
        compiler_params=pltpu.CompilerParams(
            collective_id=number, has_side_effects=True, vmem_limit_bytes=VMEM_LIMIT
        ),
    )(*operands)


def full(shape, dtype=jnp.float32):
    return jax.ShapeDtypeStruct(shape, dtype)


def forward_step(part, residual, gain):
    rows, columns = residual.shape
    return plane_call(
        forward_kernel, "forward_step", 0,
        (full((rows, columns)), full((8, rows, columns), jnp.bfloat16)),
        rows, columns, 14, True, (part, residual, gain),
    )


def backward_step(part, values, grad, gain):
    rows, columns = values.shape
    return plane_call(
        backward_kernel, "backward_step", 1,
        (full((rows, columns)), full((1, columns)), full((8, rows, columns), jnp.bfloat16)),
        rows, columns, 14, True, (part, values, grad, gain),
    )


def output_step(part, residual):
    rows, columns = residual.shape
    return plane_call(
        output_kernel, "output_step", 2, full((4, rows, columns), jnp.bfloat16),
        rows, columns, 10, True, (part, residual),
    )


def input_step(part, values, grad, gain):
    rows, columns = values.shape
    return plane_call(
        input_kernel, "input_step", 3, (full((4, rows, columns)), full((1, columns))),
        rows, columns, 10, True, (part, values, grad, gain),
    )


def gather_step(own):
    rows, columns = own.shape
    return plane_call(
        gather_kernel, "gather_step", 4, full((8, rows, columns), own.dtype),
        rows, columns, 7, False, (own,),
    )


def scatter_step(part):
    _, rows, columns = part.shape
    return plane_call(
        scatter_kernel, "scatter_step", 5, full((rows, columns), part.dtype),
        rows, columns, 7, True, (part,),
    )


def split_heads(values):
    return values.reshape(2, values.shape[0] // 2, -1, HD)


def merge_heads(values):
    return values.reshape(2 * values.shape[1], -1)


def masked_scores(queries, key_rows, allowed):
    scores = jnp.einsum(
        "bshe,bkhe->bhsk", queries, key_rows, preferred_element_type=jnp.float32
    ) * HD ** (-0.5)
    return jnp.where(allowed[:, None], scores, -1000000000.0)


def attend(queries, key_rows, value_rows, allowed):
    scores = masked_scores(queries, key_rows, allowed)
    log_total = jax.nn.logsumexp(scores, axis=-1, keepdims=True)
    attn_probs = jnp.exp(scores - log_total)
    mixed = jnp.einsum(
        "bhsk,bkhe->bshe", rounded(attn_probs), value_rows, preferred_element_type=jnp.float32
    )
    return (rounded(merge_heads(mixed)), log_total)


def attend_back(queries, key_rows, value_rows, allowed, log_total, grad_mixed):
    attn_probs = jnp.exp(masked_scores(queries, key_rows, allowed) - log_total)
    grad_probs = jnp.einsum(
        "bshe,bkhe->bhsk", grad_mixed, value_rows, preferred_element_type=jnp.float32
    )
    grad_scores = rounded(
        attn_probs * (grad_probs - jnp.sum(attn_probs * grad_probs, axis=-1, keepdims=True))
    )
    grad_queries = jnp.einsum(
        "bhsk,bkhe->bshe", grad_scores, key_rows, preferred_element_type=jnp.float32
    ) * HD ** (-0.5)
    grad_keys = jnp.einsum(
        "bhsk,bshe->bkhe", grad_scores, queries, preferred_element_type=jnp.float32
    ) * HD ** (-0.5)
    grad_values = jnp.einsum(
        "bhsk,bshe->bkhe", rounded(attn_probs), grad_mixed, preferred_element_type=jnp.float32
    )
    return tuple(rounded(merge_heads(g)) for g in (grad_queries, grad_keys, grad_values))


def gated_gelu(gate_up):
    return jax.nn.gelu(gate_up[0], approximate=True) * gate_up[1]


def dot(pattern, left, right):
    return jnp.einsum(pattern, left, right, preferred_element_type=jnp.float32)


SWAP = ((0, 1), (1, 0))


def ignore(*refs):
    del refs


def after(value, *earlier):
    anywhere = pl.BlockSpec(memory_space=pl.ANY)
    return pl.pallas_call(
        ignore,
        name="after",
        out_shape=jax.ShapeDtypeStruct(value.shape, value.dtype),
        in_specs=[anywhere] * (1 + len(earlier)),
        out_specs=anywhere,
        input_output_aliases={0: 0},
    )(value, *earlier)


def either(own, other, x, join):
    return jnp.where(x == 0, join([own, other]), join([other, own]))


def both_items(values, x):
    return either(values, lax.ppermute(values, "x", SWAP), x, jnp.concatenate)


def cut_in(weight, x):
    flat = weight.reshape(-1, weight.shape[-1])
    size = flat.shape[1] // 2
    return [lax.dynamic_slice_in_dim(flat, k * size, size, 1) for k in (x, 1 - x)]


def cut_out(weight, x, columns):
    size = weight.shape[0] // 2
    return [
        lax.dynamic_slice_in_dim(weight, k * size, size, 0).reshape(-1, columns)
        for k in (x, 1 - x)
    ]


def swap_group(pairs, x, *earlier):
    keep = jnp.concatenate([pair[0] for pair in pairs])
    give = jnp.concatenate([pair[1] for pair in pairs])
    if earlier:
        give = after(give, *earlier)
    return either(keep, lax.ppermute(give, "x", SWAP), x, jnp.stack)


def gather_group(swapped):
    return lax.all_gather(swapped, "z", axis=0, tiled=True)


def scatter_group(parts):
    return lax.psum_scatter(parts, "z", scatter_dimension=0, tiled=True)


def home_group(share, x):
    give = lax.dynamic_index_in_dim(share, 1 - x, 0, False)
    return lax.dynamic_index_in_dim(share, x, 0, False), lax.ppermute(give, "x", SWAP)


def home(pair, place, shape, axis, x):
    own, other = (half[place[0] : place[1]].reshape(shape) for half in pair)
    joined = either(own, other, x, functools.partial(jnp.concatenate, axis=axis))
    return joined.astype(jnp.float32)


def places(*sizes):
    ends = [sum(sizes[: k + 1]) for k in range(len(sizes))]
    return [(end - size, end) for end, size in zip(ends, sizes)]


def on_device(
    tokens,
    patches,
    lengths,
    patch_keep,
    norm_gains,
    self_qkv,
    self_out,
    cross_q,
    cross_kv,
    cross_out,
    patch_proj,
    ffn_in,
    ffn_out,
    cotangent,
):
    x = lax.axis_index("x")
    m = lax.axis_index("mp")
    slots, width = tokens.shape[1], tokens.shape[2]
    rows = slots // 4
    depth, patch_depth = cross_q.shape[0], patch_proj.shape[0]
    blocks = width // depth
    heads, units = self_out.shape[0] // 2, ffn_out.shape[0] // 2
    at_patch, at_qkv, at_gain = places(patch_depth, 3 * depth, 16)
    at_kv, at_q, at_self, at_cross = places(2 * depth, depth, depth, depth)

    def padded(values):
        flat = values.reshape(-1, 3 * depth)
        return jnp.pad(flat, ((0, 0), (0, 16 * heads - 3 * depth))).reshape(-1, 16, heads)

    def unpadded(values):
        return values.reshape(-1, 16 * heads)[:, : 3 * depth].reshape(-1, 3, depth)

    first = swap_group(
        [cut_in(patch_proj, x), cut_in(self_qkv, x), [padded(norm_gains)[0]] * 2], x
    )
    first_w = gather_group(first)
    token_all = both_items(after(tokens[0], first), x)
    second = swap_group(
        [
            cut_in(cross_kv, x),
            cut_in(cross_q, x),
            cut_out(self_out, x, heads),
            cut_out(cross_out, x, heads),
        ],
        x,
        token_all,
    )
    second_w = gather_group(after(second, first_w))
    patch_all = both_items(after(patches[0], second), x)
    third = swap_group([cut_in(ffn_in, x)], x, patch_all)
    fourth = swap_group([cut_out(ffn_out, x, depth)], x, third)
    grad_all = both_items(after(cotangent[0], fourth), x)

    patch_w = first_w[:, at_patch[0] : at_patch[1]].reshape(-1, heads)
    qkv_w = first_w[:, at_qkv[0] : at_qkv[1]].reshape(blocks, 3, depth, heads)
    cross_kv_w = second_w[:, at_kv[0] : at_kv[1]].reshape(blocks, 2, depth, heads)
    cross_q_w = second_w[:, at_q[0] : at_q[1]].reshape(width, heads)
    self_out_w = second_w[:, at_self[0] : at_self[1]].reshape(blocks, heads, depth)
    cross_out_w = second_w[:, at_cross[0] : at_cross[1]].reshape(blocks, heads, depth)

    gains = unpadded(first_w[:, at_gain[0] : at_gain[1]])
    gains = gains.transpose(1, 0, 2).reshape(3, width).astype(jnp.float32)
    gain_of = [gains[i : i + 1] for i in range(3)]
    facts = jnp.concatenate([patch_keep, lengths[:, None]], axis=1)
    facts = lax.all_gather(facts, "x", axis=0, tiled=True)
    patch_keep, lengths = facts[:, :-1], facts[:, -1]

    row_index = lax.broadcasted_iota(jnp.int32, (slots, slots), 0)
    col_index = lax.broadcasted_iota(jnp.int32, (slots, slots), 1)
    self_allowed = (col_index <= row_index)[None] & (col_index[None] < lengths[:, None, None])
    cross_allowed = (patch_keep > 0)[:, None, :]

    own_tokens = lax.dynamic_slice_in_dim(tokens[0], m * rows, rows, 0).astype(jnp.float32)
    own_grad = lax.dynamic_slice_in_dim(cotangent[0], m * rows, rows, 0).astype(jnp.float32)

    values = token_all.astype(jnp.float32)
    normed_self = rounded(
        values
        * lax.rsqrt(jnp.mean(values * values, axis=-1, keepdims=True) + EPS)
        * gain_of[0]
    )

    def to_blocks(partial_value):
        return rounded(partial_value).reshape(8, rows, width)

    def from_blocks(values):
        return values.reshape(8 * rows, width)

    def cut(values):
        return values.reshape(values.shape[0], blocks, depth)

    def stacked(*parts):
        return jnp.concatenate([rounded(part).reshape(blocks, -1, heads) for part in parts], axis=1)

    projected = rounded(dot("sbd,bcdf->csf", cut(normed_self), qkv_w))
    self_parts = [split_heads(projected[i]) for i in range(3)]
    mixed_self, total_self = attend(*self_parts, self_allowed)
    memory_part = rounded(dot("pk,kd->pd", patch_all, patch_w))
    memory_blocks = gather_step(memory_part)
    memory = (
        memory_blocks.reshape(2, 4, memory_part.shape[0], -1)
        .transpose(2, 1, 0, 3)
        .reshape(memory_part.shape[0], -1)
    )
    third_w = gather_group(after(third, second_w, mixed_self, memory_blocks))
    ffn_in_w = third_w.reshape(blocks, 2, depth, units)

    part = dot("sk,bkd->sbd", mixed_self, self_out_w)
    after_self, normed_cross = forward_step(to_blocks(part), own_tokens, gain_of[1])
    normed_cross = from_blocks(normed_cross)

    key_value = rounded(dot("pbd,bcdf->cpf", cut(memory), cross_kv_w))
    query_heads = split_heads(rounded(dot("sd,df->sf", normed_cross, cross_q_w)))
    cross_keys = split_heads(key_value[0])
    cross_values = split_heads(key_value[1])
    mixed_cross, total_cross = attend(query_heads, cross_keys, cross_values, cross_allowed)
    part = dot("sk,bkd->sbd", mixed_cross, cross_out_w)
    after_cross, normed_ffn = forward_step(to_blocks(part), after_self, gain_of[2])
    fourth_w = gather_group(after(fourth, third_w, normed_ffn))
    ffn_out_w = fourth_w.reshape(blocks, units, depth)
    normed_ffn = from_blocks(normed_ffn)

    gate_up = dot("sbd,bcdf->csf", cut(normed_ffn), ffn_in_w)
    hidden = rounded(gated_gelu(gate_up))
    ffn_out_part = rounded(dot("sf,sbd->bfd", hidden, cut(grad_all)))
    ffn_out_share = scatter_group(after(ffn_out_part, fourth_w))
    output_part = to_blocks(dot("sf,bfd->sbd", hidden, ffn_out_w))

    grad_hidden = dot("sbd,bfd->sf", cut(grad_all), ffn_out_w)
    grad_gate_up = rounded(jax.vjp(gated_gelu, gate_up)[1](grad_hidden)[0])
    ffn_in_part = rounded(dot("sbd,csf->bcdf", cut(normed_ffn), grad_gate_up))
    part = dot("csf,bcdf->sbd", grad_gate_up, ffn_in_w)
    grad_after_cross, gain_ffn, grad_all = backward_step(
        to_blocks(part), after_cross, own_grad, gain_of[2]
    )
    ffn_in_part = ffn_in_part.reshape(blocks, 2 * depth, units)
    ffn_in_share = scatter_group(after(ffn_in_part, ffn_out_share, grad_all))
    grad_all = from_blocks(grad_all)

    cross_out_part = dot("sk,sbd->bkd", mixed_cross, cut(grad_all))
    grad_mixed = split_heads(rounded(dot("sbd,bkd->sk", cut(grad_all), cross_out_w)))
    grad_queries, grad_keys, grad_values = attend_back(
        query_heads, cross_keys, cross_values, cross_allowed, total_cross, grad_mixed
    )
    part = dot("sf,df->sd", grad_queries, cross_q_w)
    grad_after_self, gain_cross, grad_all = backward_step(
        to_blocks(part), after_self, grad_after_cross, gain_of[1]
    )
    grad_all = from_blocks(grad_all)
    grad_key_value = jnp.stack([grad_keys, grad_values])
    second_part = stacked(
        dot("pbd,cpf->bcdf", cut(memory), grad_key_value),
        dot("sbd,sf->bdf", cut(normed_cross), grad_queries),
        cross_out_part,
    )
    self_out_part = dot("sk,sbd->bkd", mixed_self, cut(grad_all))
    grad_mixed = split_heads(rounded(dot("sbd,bkd->sk", cut(grad_all), self_out_w)))
    grad_projected = jnp.stack(attend_back(*self_parts, self_allowed, total_self, grad_mixed))
    second_share = scatter_group(after(second_part, ffn_in_share, grad_projected))

    part = rounded(dot("cpf,bcdf->pbd", grad_key_value, cross_kv_w))
    part = part.reshape(part.shape[0], 4, 2, -1).transpose(2, 1, 0, 3)
    grad_memory = scatter_step(part.reshape(8, *memory_part.shape))
    part = to_blocks(dot("csf,bcdf->sbd", grad_projected, qkv_w))
    grad_input, gain_self = input_step(part, own_tokens, grad_after_self, gain_of[0])
    gains_part = jnp.concatenate([gain_self, gain_cross, gain_ffn], axis=0)
    gains_part = gains_part.reshape(3, blocks, depth).transpose(1, 0, 2)
    patch_cut = patch_all.reshape(patch_all.shape[0], blocks, patch_depth)
    first_part = stacked(
        dot("pbk,pd->bkd", patch_cut, grad_memory),
        dot("sbd,csf->bcdf", cut(normed_self), grad_projected),
        self_out_part,
        padded(gains_part),
    )
    first_part = after(first_part, second_share, grad_input)
    first_share = scatter_group(first_part)
    output = output_step(after(output_part, first_part), after_cross)

    pair = home_group(after(ffn_out_share, first_part), x)
    grad_ffn_out = home(pair, (0, units), (units, depth), 0, x)
    pair = home_group(after(ffn_in_share, first_part), x)
    grad_ffn_in = home(pair, (0, 2 * depth), (2, depth, units), 2, x)
    pair = home_group(after(second_share, first_part), x)
    at_kv, at_q, at_cross = places(2 * depth, depth, depth)
    grad_cross_kv = home(pair, at_kv, (2, depth, heads), 2, x)
    grad_cross_q = home(pair, at_q, (depth, heads), 1, x)
    grad_cross_out = home(pair, at_cross, (heads, depth), 0, x)
    pair = home_group(first_share, x)
    at_patch, at_qkv, at_self, at_gain = places(patch_depth, 3 * depth, depth, 16)
    grad_patch = home(pair, at_patch, (patch_depth, heads), 1, x)
    grad_self_qkv = home(pair, at_qkv, (3, depth, heads), 2, x)
    grad_self_out = home(pair, at_self, (heads, depth), 0, x)
    grad_gains = sum(half[at_gain[0] : at_gain[1]].astype(jnp.float32) for half in pair)
    grad_gains = lax.psum(unpadded(grad_gains)[0], "mp")
    return (
        output.reshape(1, slots, width),
        grad_input.reshape(1, slots, width),
        grad_gains,
        grad_self_qkv,
        grad_self_out,
        grad_cross_q,
        grad_cross_kv,
        grad_cross_out,
        grad_patch,
        grad_ffn_in,
        grad_ffn_out,
    )


def solution(mesh):
    batch, parts = mesh.shape["batch"], mesh.shape["mp"]
    planes = Mesh(mesh.devices.reshape(batch // 2, 2, parts), ("z", "x", "mp"))
    b = ("z", "x")
    weights = (
        P(None, b, "mp"),
        P("mp", b),
        P(b, "mp"),
        P(None, b, "mp"),
        P("mp", b),
        P(b, "mp"),
        P(None, b, "mp"),
        P("mp", b),
    )
    row = P(b, None, None)
    return jax.shard_map(
        on_device,
        mesh=planes,
        in_specs=(row, row, P(b), P(b, None), P(None, b)) + weights + (row,),
        out_specs=(row, row, P(None, b)) + weights,
        check_vma=False,
    )
```

```python
import functools

import jax
import jax.numpy as jnp
from jax import lax
from jax.experimental import pallas as pl
from jax.experimental.pallas import tpu as pltpu
from jax.sharding import Mesh
from jax.sharding import PartitionSpec as P

HD = 64
EPS = 1e-06
RELATIVE = ((1, 1), (1, 0), (0, 1), (0, 0))
VMEM_LIMIT = 48 * 2**20


def rounded(values):
    return values.astype(jnp.bfloat16)


def flip(value, by):
    return value + by * (1 - 2 * value)


class Plane:
    def __init__(self):
        self.x = lax.axis_index("x")
        part = lax.axis_index("mp")
        self.y = part // 2
        self.c = part % 2

    def device(self, dx, dy, dc):
        return {"x": flip(self.x, dx), "mp": flip(self.y, dy) * 2 + flip(self.c, dc)}

    def block(self, dx, dy, dc):
        return (flip(self.x, dx) * 2 + flip(self.y, dy)) * 2 + flip(self.c, dc)

    def greet(self, relations, line=None):
        barrier = pltpu.get_barrier_semaphore()
        for relation in relations:
            pl.semaphore_signal(
                barrier, inc=1, device_id=self.device(*relation), device_id_type=pl.DeviceIdType.MESH
            )
        if line is None:
            pl.semaphore_wait(barrier, len(relations))
        else:
            line.greet(barrier)
            pl.semaphore_wait(barrier, len(relations) + line.partners)

    def send(self, src, dst, sems, slot, relation):
        copy = pltpu.make_async_remote_copy(
            src_ref=src,
            dst_ref=dst,
            send_sem=sems.at[0, slot],
            recv_sem=sems.at[1, slot],
            device_id=self.device(*relation),
            device_id_type=pl.DeviceIdType.MESH,
        )
        copy.start()
        return copy


class Line:
    def __init__(self, count, at, sems):
        self.z = lax.axis_index("z")
        self.count, self.at, self.sems = count, at, sems
        self.partners = (self.z > 0).astype(jnp.int32) + (self.z < self.count - 1).astype(jnp.int32)

    def greet(self, barrier):
        for there, step in ((self.z > 0, -1), (self.z < self.count - 1, 1)):

            @pl.when(there)
            def signal(step=step):
                pl.semaphore_signal(
                    barrier,
                    inc=1,
                    device_id={"z": self.z + step},
                    device_id_type=pl.DeviceIdType.MESH,
                )

    def copy(self, block, step, way):
        at = self.at(jnp.clip(block, 0, self.count - 1))
        return pltpu.make_async_remote_copy(
            src_ref=at,
            dst_ref=at,
            send_sem=self.sems.at[0, way, step],
            recv_sem=self.sems.at[1, way, step],
            device_id={"z": jnp.clip(self.z + (1 - 2 * way), 0, self.count - 1)},
            device_id_type=pl.DeviceIdType.MESH,
        )

    def sent(self, step, way):
        block = self.z - step * (1 - 2 * way)
        last = self.count - 1
        goes = (self.z < last) & (block >= 0) if way == 0 else (self.z > 0) & (block <= last)
        return block, goes

    def start(self, step):
        for way in (0, 1):
            block, goes = self.sent(step, way)

            @pl.when(goes)
            def begin(block=block, way=way):
                self.copy(block, step, way).start()

    def arrive(self, step):
        for way in (0, 1):
            block = self.z - (step + 1) * (1 - 2 * way)

            @pl.when((block >= 0) & (block < self.count))
            def wait(block=block, way=way):
                self.copy(block, step, way).wait_recv()

    def onward(self, step):
        self.arrive(step)
        if step + 1 < self.count - 1:
            self.start(step + 1)

    def finish(self):
        for step in range(self.count - 1):
            for way in (0, 1):
                block, goes = self.sent(step, way)

                @pl.when(goes)
                def wait(block=block, way=way, step=step):
                    self.copy(block, step, way).wait_send()


ALL_RELATIONS = ((0, 0, 1), (1, 1, 0), (1, 0, 0), (0, 1, 0))
ROW_RELATIONS = ((0, 0, 1), (0, 1, 0))


def reduce_blocks(plane, part, from_core, to_chip, from_chip, sems):
    pair = [
        plane.send(part.at[plane.block(dx, dy, 1)], from_core.at[i], sems, i, (0, 0, 1))
        for i, (dx, dy) in enumerate(RELATIVE)
    ]
    across = []
    for i, (dx, dy) in enumerate(RELATIVE):
        pair[i].wait_recv()
        both = part[plane.block(dx, dy, 0)].astype(jnp.float32) + from_core[i].astype(jnp.float32)
        if i < 3:
            to_chip[i] = rounded(both)
            across.append(plane.send(to_chip.at[i], from_chip.at[i], sems, 4 + i, (dx, dy, 0)))
    for i in (2, 1, 0):
        across[i].wait_recv()
        both = both + from_chip[i].astype(jnp.float32)
    for copy in pair + across:
        copy.wait_send()
    return both


def gather_blocks(plane, out, sems, first):
    mine = plane.block(0, 0, 0)
    sends = [
        plane.send(out.at[mine], out.at[mine], sems, first + i, (dx, dy, 0))
        for i, (dx, dy) in enumerate(RELATIVE[:3])
    ]
    sends.append(plane.send(out.at[mine], out.at[mine], sems, first + 3, (0, 0, 1)))
    for i in (2, 1, 0):
        dx, dy = RELATIVE[i]
        theirs = plane.block(dx, dy, 0)
        sends[i].wait_recv()
        sends.append(plane.send(out.at[theirs], out.at[theirs], sems, first + 4 + i, (0, 0, 1)))
    for copy in sends[3:]:
        copy.wait_recv()
    for copy in sends:
        copy.wait_send()


def gather_rows(plane, out, sems, first):
    mine = plane.y * 2 + plane.c
    theirs = flip(plane.y, 1) * 2 + plane.c
    over = plane.send(out.at[mine], out.at[mine], sems, first, (0, 1, 0))
    beside = plane.send(out.at[mine], out.at[mine], sems, first + 1, (0, 0, 1))
    over.wait_recv()
    onward = plane.send(out.at[theirs], out.at[theirs], sems, first + 2, (0, 0, 1))
    beside.wait_recv()
    onward.wait_recv()
    for copy in (over, beside, onward):
        copy.wait_send()


def forward_kernel(part, residual, gain, after, normed, from_core, to_chip, from_chip, sems):
    plane = Plane()
    plane.greet(ALL_RELATIONS)
    values = residual[...] + reduce_blocks(plane, part, from_core, to_chip, from_chip, sems)
    after[...] = values
    scale = lax.rsqrt(jnp.mean(values * values, axis=-1, keepdims=True) + EPS)
    normed[plane.block(0, 0, 0)] = rounded(values * scale * gain[...])
    gather_blocks(plane, normed, sems, 7)


def back_values(values, gain, grad):
    scale = lax.rsqrt(jnp.mean(values * values, axis=-1, keepdims=True) + EPS)
    gain_part = jnp.sum(grad * values * scale, axis=0, keepdims=True)
    scaled = grad * gain
    side = scale * scaled - values * (scale * scale * scale) * jnp.mean(
        scaled * values, axis=-1, keepdims=True
    )
    return side, gain_part


def backward_kernel(
    part, values, grad, gain, grad_out, gain_part, grad_all, from_core, to_chip, from_chip, sems
):
    plane = Plane()
    plane.greet(ALL_RELATIONS)
    total = reduce_blocks(plane, part, from_core, to_chip, from_chip, sems)
    side, gain_sum = back_values(values[...], gain[...], total)
    gain_part[...] = gain_sum
    result = grad[...] + side
    grad_out[...] = result
    grad_all[plane.block(0, 0, 0)] = rounded(result)
    gather_blocks(plane, grad_all, sems, 7)


def output_kernel(part, residual, out, from_core, to_chip, from_chip, sems):
    plane = Plane()
    plane.greet(ALL_RELATIONS)
    values = residual[...] + reduce_blocks(plane, part, from_core, to_chip, from_chip, sems)
    out[plane.y * 2 + plane.c] = rounded(values)
    gather_rows(plane, out, sems, 7)


def input_kernel(part, values, grad, gain, out, gain_part, from_core, to_chip, from_chip, sems):
    plane = Plane()
    plane.greet(ALL_RELATIONS)
    total = reduce_blocks(plane, part, from_core, to_chip, from_chip, sems)
    side, gain_sum = back_values(values[...], gain[...], total)
    gain_part[...] = gain_sum
    out[plane.y * 2 + plane.c] = grad[...] + side
    gather_rows(plane, out, sems, 7)


def weights_kernel(count, others, keep, give, *refs):
    sources, out, received = refs[:others], refs[others], refs[others + 1 : 2 * others + 1]
    swap_sems, own_sems, other_sems = refs[2 * others + 1 :]
    plane = Plane()
    own = Line(count, lambda block: out.at[block, plane.x], own_sems)
    other = Line(count, lambda block: out.at[block, 1 - plane.x], other_sems)
    plane.greet(((1, 0, 0),), own)
    swap = plane.send(give, out.at[own.z, plane.x], swap_sems, 0, (1, 0, 0))
    out[own.z, plane.x] = keep[...]
    own.start(0)
    swaps = [
        plane.send(sources[i], received[i], swap_sems, 1 + i, (1, 0, 0)) for i in range(others)
    ]
    swap.wait_recv()
    other.start(0)
    for step in range(count - 1):
        own.onward(step)
        other.onward(step)
    for copy in swaps:
        copy.wait()
    swap.wait_send()
    own.finish()
    other.finish()


def gather_kernel(own, out, sems):
    plane = Plane()
    plane.greet(ALL_RELATIONS)
    out[plane.block(0, 0, 0)] = own[...]
    gather_blocks(plane, out, sems, 0)


def scatter_kernel(part, out, from_core, to_chip, from_chip, sems):
    plane = Plane()
    plane.greet(ALL_RELATIONS)
    out[...] = rounded(reduce_blocks(plane, part, from_core, to_chip, from_chip, sems))


def plane_call(kernel, name, number, outs, rows, columns, copies, reduces, operands):
    whole = pl.BlockSpec(memory_space=pltpu.VMEM)
    scratch = []
    if reduces:
        scratch = [
            pltpu.VMEM((4, rows, columns), jnp.bfloat16),
            pltpu.VMEM((3, rows, columns), jnp.bfloat16),
            pltpu.VMEM((3, rows, columns), jnp.bfloat16),
        ]
    scratch.append(pltpu.SemaphoreType.DMA((2, copies)))
    return pl.pallas_call(
        kernel,
        name=name,
        out_shape=outs,
        in_specs=[whole] * len(operands),
        out_specs=jax.tree.map(lambda _: whole, outs),
        scratch_shapes=scratch,
        compiler_params=pltpu.CompilerParams(
            collective_id=number, has_side_effects=True, vmem_limit_bytes=VMEM_LIMIT
        ),
    )(*operands)


def full(shape, dtype=jnp.float32):
    return jax.ShapeDtypeStruct(shape, dtype)


def forward_step(part, residual, gain):
    rows, columns = residual.shape
    return plane_call(
        forward_kernel, "forward_step", 0,
        (full((rows, columns)), full((8, rows, columns), jnp.bfloat16)),
        rows, columns, 14, True, (part, residual, gain),
    )


def backward_step(part, values, grad, gain):
    rows, columns = values.shape
    return plane_call(
        backward_kernel, "backward_step", 1,
        (full((rows, columns)), full((1, columns)), full((8, rows, columns), jnp.bfloat16)),
        rows, columns, 14, True, (part, values, grad, gain),
    )


def output_step(part, residual):
    rows, columns = residual.shape
    return plane_call(
        output_kernel, "output_step", 2, full((4, rows, columns), jnp.bfloat16),
        rows, columns, 10, True, (part, residual),
    )


def input_step(part, values, grad, gain):
    rows, columns = values.shape
    return plane_call(
        input_kernel, "input_step", 3, (full((4, rows, columns)), full((1, columns))),
        rows, columns, 10, True, (part, values, grad, gain),
    )


def weights_step(keep, give, sources, planes):
    anywhere = pl.BlockSpec(memory_space=pl.ANY)
    whole = pl.BlockSpec(memory_space=pltpu.VMEM)
    outs = [full((planes, 2) + keep.shape, keep.dtype)]
    outs += [full(source.shape, source.dtype) for source in sources]
    return pl.pallas_call(
        functools.partial(weights_kernel, planes, len(sources)),
        name="weights_step",
        out_shape=outs,
        in_specs=[whole, whole] + [anywhere] * len(sources),
        out_specs=[whole] + [anywhere] * len(sources),
        scratch_shapes=[
            pltpu.SemaphoreType.DMA((2, 1 + len(sources))),
            pltpu.SemaphoreType.DMA((2, 2, planes - 1)),
            pltpu.SemaphoreType.DMA((2, 2, planes - 1)),
        ],
        compiler_params=pltpu.CompilerParams(
            collective_id=6, has_side_effects=True, vmem_limit_bytes=VMEM_LIMIT
        ),
    )(keep, give, *sources)


def gather_step(own):
    rows, columns = own.shape
    return plane_call(
        gather_kernel, "gather_step", 4, full((8, rows, columns), own.dtype),
        rows, columns, 7, False, (own,),
    )


def scatter_step(part):
    _, rows, columns = part.shape
    return plane_call(
        scatter_kernel, "scatter_step", 5, full((rows, columns), part.dtype),
        rows, columns, 7, True, (part,),
    )


def split_heads(values):
    return values.reshape(2, values.shape[0] // 2, -1, HD)


def merge_heads(values):
    return values.reshape(2 * values.shape[1], -1)


def masked_scores(queries, key_rows, allowed):
    scores = jnp.einsum(
        "bshe,bkhe->bhsk", queries, key_rows, preferred_element_type=jnp.float32
    ) * HD ** (-0.5)
    return jnp.where(allowed[:, None], scores, -1000000000.0)


def attend(queries, key_rows, value_rows, allowed):
    scores = masked_scores(queries, key_rows, allowed)
    log_total = jax.nn.logsumexp(scores, axis=-1, keepdims=True)
    attn_probs = jnp.exp(scores - log_total)
    mixed = jnp.einsum(
        "bhsk,bkhe->bshe", rounded(attn_probs), value_rows, preferred_element_type=jnp.float32
    )
    return (rounded(merge_heads(mixed)), log_total)


def attend_back(queries, key_rows, value_rows, allowed, log_total, grad_mixed):
    attn_probs = jnp.exp(masked_scores(queries, key_rows, allowed) - log_total)
    grad_probs = jnp.einsum(
        "bshe,bkhe->bhsk", grad_mixed, value_rows, preferred_element_type=jnp.float32
    )
    grad_scores = rounded(
        attn_probs * (grad_probs - jnp.sum(attn_probs * grad_probs, axis=-1, keepdims=True))
    )
    grad_queries = jnp.einsum(
        "bhsk,bkhe->bshe", grad_scores, key_rows, preferred_element_type=jnp.float32
    ) * HD ** (-0.5)
    grad_keys = jnp.einsum(
        "bhsk,bshe->bkhe", grad_scores, queries, preferred_element_type=jnp.float32
    ) * HD ** (-0.5)
    grad_values = jnp.einsum(
        "bhsk,bshe->bkhe", rounded(attn_probs), grad_mixed, preferred_element_type=jnp.float32
    )
    return tuple(rounded(merge_heads(g)) for g in (grad_queries, grad_keys, grad_values))


def gated_gelu(gate_up):
    return jax.nn.gelu(gate_up[0], approximate=True) * gate_up[1]


def dot(pattern, left, right):
    return jnp.einsum(pattern, left, right, preferred_element_type=jnp.float32)


SWAP = ((0, 1), (1, 0))


def ignore(*refs):
    del refs


def after(value, *earlier):
    anywhere = pl.BlockSpec(memory_space=pl.ANY)
    return pl.pallas_call(
        ignore,
        name="after",
        out_shape=jax.ShapeDtypeStruct(value.shape, value.dtype),
        in_specs=[anywhere] * (1 + len(earlier)),
        out_specs=anywhere,
        input_output_aliases={0: 0},
    )(value, *earlier)


def either(own, other, x, join):
    return jnp.where(x == 0, join([own, other]), join([other, own]))


def cut_in(weight, x):
    flat = weight.reshape(-1, weight.shape[-1])
    size = flat.shape[1] // 2
    return [lax.dynamic_slice_in_dim(flat, k * size, size, 1) for k in (x, 1 - x)]


def cut_out(weight, x, columns):
    size = weight.shape[0] // 2
    return [
        lax.dynamic_slice_in_dim(weight, k * size, size, 0).reshape(-1, columns)
        for k in (x, 1 - x)
    ]


def gather_group(swapped):
    return lax.all_gather(swapped, "z", axis=0, tiled=True)


def scatter_group(parts):
    return lax.psum_scatter(parts, "z", scatter_dimension=0, tiled=True)


def home_group(share, x):
    give = lax.dynamic_index_in_dim(share, 1 - x, 0, False)
    return lax.dynamic_index_in_dim(share, x, 0, False), lax.ppermute(give, "x", SWAP)


def home(pair, place, shape, axis, x):
    own, other = (half[place[0] : place[1]].reshape(shape) for half in pair)
    joined = either(own, other, x, functools.partial(jnp.concatenate, axis=axis))
    return joined.astype(jnp.float32)


def places(*sizes):
    ends = [sum(sizes[: k + 1]) for k in range(len(sizes))]
    return [(end - size, end) for end, size in zip(ends, sizes)]


def on_device(
    tokens,
    patches,
    lengths,
    patch_keep,
    norm_gains,
    self_qkv,
    self_out,
    cross_q,
    cross_kv,
    cross_out,
    patch_proj,
    ffn_in,
    ffn_out,
    cotangent,
):
    x = lax.axis_index("x")
    m = lax.axis_index("mp")
    slots, width = tokens.shape[1], tokens.shape[2]
    rows = slots // 4
    depth, patch_depth = cross_q.shape[0], patch_proj.shape[0]
    blocks = width // depth
    heads, units = self_out.shape[0] // 2, ffn_out.shape[0] // 2
    at_patch, at_qkv, at_gain = places(patch_depth, 3 * depth, 16)
    at_kv, at_q, at_self, at_cross = places(2 * depth, depth, depth, depth)

    def padded(values):
        flat = values.reshape(-1, 3 * depth)
        return jnp.pad(flat, ((0, 0), (0, 16 * heads - 3 * depth))).reshape(-1, 16, heads)

    def unpadded(values):
        return values.reshape(-1, 16 * heads)[:, : 3 * depth].reshape(-1, 3, depth)

    early = [
        cut_in(patch_proj, x),
        cut_in(self_qkv, x),
        [padded(norm_gains)[0]] * 2,
        cut_in(cross_kv, x),
        cut_in(cross_q, x),
        cut_out(self_out, x, heads),
        cut_out(cross_out, x, heads),
    ]
    keep, give = (jnp.concatenate([pair[k] for pair in early]) for k in (0, 1))
    third, fourth = cut_in(ffn_in, x), cut_out(ffn_out, x, depth)
    facts = jnp.concatenate([patch_keep, lengths[:, None]], axis=1)
    facts = jnp.pad(facts, ((0, 7), (0, 127)))
    sources = (third[1], tokens[0], patches[0], fourth[1], cotangent[0], facts)
    early_w, third_other, token_other, patch_other, fourth_other, grad_other, facts_other = (
        weights_step(keep, give, sources, blocks // 2)
    )
    third = either(third[0], third_other, x, jnp.stack)
    fourth = either(fourth[0], fourth_other, x, jnp.stack)
    token_all = either(tokens[0], token_other, x, jnp.concatenate)
    patch_all = either(patches[0], patch_other, x, jnp.concatenate)
    grad_all = either(cotangent[0], grad_other, x, jnp.concatenate)
    third_w = gather_group(third)
    early_w = early_w.reshape(blocks, *keep.shape)
    split = at_gain[1]
    first_w, second_w = early_w[:, :split], early_w[:, split:]

    patch_w = first_w[:, at_patch[0] : at_patch[1]].reshape(-1, heads)
    qkv_w = first_w[:, at_qkv[0] : at_qkv[1]].reshape(blocks, 3, depth, heads)
    cross_kv_w = second_w[:, at_kv[0] : at_kv[1]].reshape(blocks, 2, depth, heads)
    cross_q_w = second_w[:, at_q[0] : at_q[1]].reshape(width, heads)
    self_out_w = second_w[:, at_self[0] : at_self[1]].reshape(blocks, heads, depth)
    cross_out_w = second_w[:, at_cross[0] : at_cross[1]].reshape(blocks, heads, depth)

    gains = unpadded(first_w[:, at_gain[0] : at_gain[1]])
    gains = gains.transpose(1, 0, 2).reshape(3, width).astype(jnp.float32)
    gain_of = [gains[i : i + 1] for i in range(3)]
    facts = either(facts[:1], facts_other[:1], x, jnp.concatenate)
    length_at = patch_keep.shape[1]
    patch_keep, lengths = facts[:, :length_at], facts[:, length_at]

    row_index = lax.broadcasted_iota(jnp.int32, (slots, slots), 0)
    col_index = lax.broadcasted_iota(jnp.int32, (slots, slots), 1)
    self_allowed = (col_index <= row_index)[None] & (col_index[None] < lengths[:, None, None])
    cross_allowed = (patch_keep > 0)[:, None, :]

    own_tokens = lax.dynamic_slice_in_dim(tokens[0], m * rows, rows, 0).astype(jnp.float32)
    own_grad = lax.dynamic_slice_in_dim(cotangent[0], m * rows, rows, 0).astype(jnp.float32)

    values = token_all.astype(jnp.float32)
    normed_self = rounded(
        values
        * lax.rsqrt(jnp.mean(values * values, axis=-1, keepdims=True) + EPS)
        * gain_of[0]
    )

    def to_blocks(partial_value):
        return rounded(partial_value).reshape(8, rows, width)

    def from_blocks(values):
        return values.reshape(8 * rows, width)

    def cut(values):
        return values.reshape(values.shape[0], blocks, depth)

    def stacked(*parts):
        return jnp.concatenate([rounded(part).reshape(blocks, -1, heads) for part in parts], axis=1)

    projected = rounded(dot("sbd,bcdf->csf", cut(normed_self), qkv_w))
    self_parts = [split_heads(projected[i]) for i in range(3)]
    mixed_self, total_self = attend(*self_parts, self_allowed)
    memory_part = rounded(dot("pk,kd->pd", patch_all, patch_w))
    memory_blocks = gather_step(memory_part)
    memory = (
        memory_blocks.reshape(2, 4, memory_part.shape[0], -1)
        .transpose(2, 1, 0, 3)
        .reshape(memory_part.shape[0], -1)
    )
    ffn_in_w = third_w.reshape(blocks, 2, depth, units)

    part = dot("sk,bkd->sbd", mixed_self, self_out_w)
    after_self, normed_cross = forward_step(to_blocks(part), own_tokens, gain_of[1])
    normed_cross = from_blocks(normed_cross)

    key_value = rounded(dot("pbd,bcdf->cpf", cut(memory), cross_kv_w))
    query_heads = split_heads(rounded(dot("sd,df->sf", normed_cross, cross_q_w)))
    fourth_w = gather_group(after(fourth, third_w, normed_cross, key_value))
    cross_keys = split_heads(key_value[0])
    cross_values = split_heads(key_value[1])
    mixed_cross, total_cross = attend(query_heads, cross_keys, cross_values, cross_allowed)
    part = dot("sk,bkd->sbd", mixed_cross, cross_out_w)
    after_cross, normed_ffn = forward_step(to_blocks(part), after_self, gain_of[2])
    ffn_out_w = fourth_w.reshape(blocks, units, depth)
    normed_ffn = from_blocks(normed_ffn)

    gate_up = dot("sbd,bcdf->csf", cut(normed_ffn), ffn_in_w)
    hidden = rounded(gated_gelu(gate_up))
    ffn_out_part = rounded(dot("sf,sbd->bfd", hidden, cut(grad_all)))
    ffn_out_share = scatter_group(after(ffn_out_part, fourth_w))
    output_part = to_blocks(dot("sf,bfd->sbd", hidden, ffn_out_w))

    grad_hidden = dot("sbd,bfd->sf", cut(grad_all), ffn_out_w)
    grad_gate_up = rounded(jax.vjp(gated_gelu, gate_up)[1](grad_hidden)[0])
    ffn_in_part = rounded(dot("sbd,csf->bcdf", cut(normed_ffn), grad_gate_up))
    part = dot("csf,bcdf->sbd", grad_gate_up, ffn_in_w)
    grad_after_cross, gain_ffn, grad_all = backward_step(
        to_blocks(part), after_cross, own_grad, gain_of[2]
    )
    ffn_in_part = ffn_in_part.reshape(blocks, 2 * depth, units)
    ffn_in_share = scatter_group(after(ffn_in_part, ffn_out_share, grad_all))
    grad_all = from_blocks(grad_all)

    cross_out_part = dot("sk,sbd->bkd", mixed_cross, cut(grad_all))
    grad_mixed = split_heads(rounded(dot("sbd,bkd->sk", cut(grad_all), cross_out_w)))
    grad_queries, grad_keys, grad_values = attend_back(
        query_heads, cross_keys, cross_values, cross_allowed, total_cross, grad_mixed
    )
    part = dot("sf,df->sd", grad_queries, cross_q_w)
    grad_after_self, gain_cross, grad_all = backward_step(
        to_blocks(part), after_self, grad_after_cross, gain_of[1]
    )
    grad_all = from_blocks(grad_all)
    grad_key_value = jnp.stack([grad_keys, grad_values])
    second_part = stacked(
        dot("pbd,cpf->bcdf", cut(memory), grad_key_value),
        dot("sbd,sf->bdf", cut(normed_cross), grad_queries),
        cross_out_part,
    )
    self_out_part = dot("sk,sbd->bkd", mixed_self, cut(grad_all))
    grad_mixed = split_heads(rounded(dot("sbd,bkd->sk", cut(grad_all), self_out_w)))
    grad_projected = jnp.stack(attend_back(*self_parts, self_allowed, total_self, grad_mixed))
    second_share = scatter_group(after(second_part, ffn_in_share, grad_projected))

    part = rounded(dot("cpf,bcdf->pbd", grad_key_value, cross_kv_w))
    part = part.reshape(part.shape[0], 4, 2, -1).transpose(2, 1, 0, 3)
    grad_memory = scatter_step(part.reshape(8, *memory_part.shape))
    part = to_blocks(dot("csf,bcdf->sbd", grad_projected, qkv_w))
    grad_input, gain_self = input_step(part, own_tokens, grad_after_self, gain_of[0])
    gains_part = jnp.concatenate([gain_self, gain_cross, gain_ffn], axis=0)
    gains_part = gains_part.reshape(3, blocks, depth).transpose(1, 0, 2)
    patch_cut = patch_all.reshape(patch_all.shape[0], blocks, patch_depth)
    first_part = stacked(
        dot("pbk,pd->bkd", patch_cut, grad_memory),
        dot("sbd,csf->bcdf", cut(normed_self), grad_projected),
        self_out_part,
        padded(gains_part),
    )
    first_part = after(first_part, second_share, grad_input)
    first_share = scatter_group(first_part)
    output = output_step(after(output_part, first_part), after_cross)

    pair = home_group(after(ffn_out_share, first_part), x)
    grad_ffn_out = home(pair, (0, units), (units, depth), 0, x)
    pair = home_group(after(ffn_in_share, first_part), x)
    grad_ffn_in = home(pair, (0, 2 * depth), (2, depth, units), 2, x)
    pair = home_group(after(second_share, first_part), x)
    at_kv, at_q, at_cross = places(2 * depth, depth, depth)
    grad_cross_kv = home(pair, at_kv, (2, depth, heads), 2, x)
    grad_cross_q = home(pair, at_q, (depth, heads), 1, x)
    grad_cross_out = home(pair, at_cross, (heads, depth), 0, x)
    pair = home_group(first_share, x)
    at_patch, at_qkv, at_self, at_gain = places(patch_depth, 3 * depth, depth, 16)
    grad_patch = home(pair, at_patch, (patch_depth, heads), 1, x)
    grad_self_qkv = home(pair, at_qkv, (3, depth, heads), 2, x)
    grad_self_out = home(pair, at_self, (heads, depth), 0, x)
    grad_gains = sum(half[at_gain[0] : at_gain[1]].astype(jnp.float32) for half in pair)
    grad_gains = lax.psum(unpadded(grad_gains)[0], "mp")
    return (
        output.reshape(1, slots, width),
        grad_input.reshape(1, slots, width),
        grad_gains,
        grad_self_qkv,
        grad_self_out,
        grad_cross_q,
        grad_cross_kv,
        grad_cross_out,
        grad_patch,
        grad_ffn_in,
        grad_ffn_out,
    )


def solution(mesh):
    batch, parts = mesh.shape["batch"], mesh.shape["mp"]
    planes = Mesh(mesh.devices.reshape(batch // 2, 2, parts), ("z", "x", "mp"))
    b = ("z", "x")
    weights = (
        P(None, b, "mp"),
        P("mp", b),
        P(b, "mp"),
        P(None, b, "mp"),
        P("mp", b),
        P(b, "mp"),
        P(None, b, "mp"),
        P("mp", b),
    )
    row = P(b, None, None)
    return jax.shard_map(
        on_device,
        mesh=planes,
        in_specs=(row, row, P(b), P(b, None), P(None, b)) + weights + (row,),
        out_specs=(row, row, P(None, b)) + weights,
        check_vma=False,
    )
```

```python
import functools

import jax
import jax.numpy as jnp
from jax import lax
from jax.experimental import pallas as pl
from jax.experimental.pallas import tpu as pltpu
from jax.sharding import Mesh
from jax.sharding import PartitionSpec as P

HD = 64
EPS = 1e-06
RELATIVE = ((1, 1), (1, 0), (0, 1), (0, 0))
VMEM_LIMIT = 48 * 2**20


def rounded(values):
    return values.astype(jnp.bfloat16)


def flip(value, by):
    return value + by * (1 - 2 * value)


class Plane:
    def __init__(self):
        self.x = lax.axis_index("x")
        part = lax.axis_index("mp")
        self.y = part // 2
        self.c = part % 2

    def device(self, dx, dy, dc):
        return {"x": flip(self.x, dx), "mp": flip(self.y, dy) * 2 + flip(self.c, dc)}

    def block(self, dx, dy, dc):
        return (flip(self.x, dx) * 2 + flip(self.y, dy)) * 2 + flip(self.c, dc)

    def greet(self, relations, line=None):
        barrier = pltpu.get_barrier_semaphore()
        for relation in relations:
            pl.semaphore_signal(
                barrier, inc=1, device_id=self.device(*relation), device_id_type=pl.DeviceIdType.MESH
            )
        if line is None:
            pl.semaphore_wait(barrier, len(relations))
        else:
            line.greet(barrier)
            pl.semaphore_wait(barrier, len(relations) + line.partners)

    def send(self, src, dst, sems, slot, relation):
        copy = pltpu.make_async_remote_copy(
            src_ref=src,
            dst_ref=dst,
            send_sem=sems.at[0, slot],
            recv_sem=sems.at[1, slot],
            device_id=self.device(*relation),
            device_id_type=pl.DeviceIdType.MESH,
        )
        copy.start()
        return copy


class Line:
    def __init__(self, count, at, sems):
        self.z = lax.axis_index("z")
        self.count, self.at, self.sems = count, at, sems
        self.partners = (self.z > 0).astype(jnp.int32) + (self.z < self.count - 1).astype(jnp.int32)

    def greet(self, barrier):
        for there, step in ((self.z > 0, -1), (self.z < self.count - 1, 1)):

            @pl.when(there)
            def signal(step=step):
                pl.semaphore_signal(
                    barrier,
                    inc=1,
                    device_id={"z": self.z + step},
                    device_id_type=pl.DeviceIdType.MESH,
                )

    def copy(self, block, step, way):
        at = self.at(jnp.clip(block, 0, self.count - 1))
        return pltpu.make_async_remote_copy(
            src_ref=at,
            dst_ref=at,
            send_sem=self.sems.at[0, way, step],
            recv_sem=self.sems.at[1, way, step],
            device_id={"z": jnp.clip(self.z + (1 - 2 * way), 0, self.count - 1)},
            device_id_type=pl.DeviceIdType.MESH,
        )

    def sent(self, step, way):
        block = self.z - step * (1 - 2 * way)
        last = self.count - 1
        goes = (self.z < last) & (block >= 0) if way == 0 else (self.z > 0) & (block <= last)
        return block, goes

    def start(self, step):
        for way in (0, 1):
            block, goes = self.sent(step, way)

            @pl.when(goes)
            def begin(block=block, way=way):
                self.copy(block, step, way).start()

    def arrive(self, step):
        for way in (0, 1):
            block = self.z - (step + 1) * (1 - 2 * way)

            @pl.when((block >= 0) & (block < self.count))
            def wait(block=block, way=way):
                self.copy(block, step, way).wait_recv()

    def onward(self, step):
        self.arrive(step)
        if step + 1 < self.count - 1:
            self.start(step + 1)

    def finish(self):
        for step in range(self.count - 1):
            for way in (0, 1):
                block, goes = self.sent(step, way)

                @pl.when(goes)
                def wait(block=block, way=way, step=step):
                    self.copy(block, step, way).wait_send()


ALL_RELATIONS = ((0, 0, 1), (1, 1, 0), (1, 0, 0), (0, 1, 0))
ROW_RELATIONS = ((0, 0, 1), (0, 1, 0))


def reduce_blocks(plane, part, from_core, to_chip, from_chip, sems):
    pair = [
        plane.send(part.at[plane.block(dx, dy, 1)], from_core.at[i], sems, i, (0, 0, 1))
        for i, (dx, dy) in enumerate(RELATIVE)
    ]
    across = []
    for i, (dx, dy) in enumerate(RELATIVE):
        pair[i].wait_recv()
        both = part[plane.block(dx, dy, 0)].astype(jnp.float32) + from_core[i].astype(jnp.float32)
        if i < 3:
            to_chip[i] = rounded(both)
            across.append(plane.send(to_chip.at[i], from_chip.at[i], sems, 4 + i, (dx, dy, 0)))
    for i in (2, 1, 0):
        across[i].wait_recv()
        both = both + from_chip[i].astype(jnp.float32)
    for copy in pair + across:
        copy.wait_send()
    return both


def gather_blocks(plane, out, sems, first):
    mine = plane.block(0, 0, 0)
    sends = [
        plane.send(out.at[mine], out.at[mine], sems, first + i, (dx, dy, 0))
        for i, (dx, dy) in enumerate(RELATIVE[:3])
    ]
    sends.append(plane.send(out.at[mine], out.at[mine], sems, first + 3, (0, 0, 1)))
    for i in (2, 1, 0):
        dx, dy = RELATIVE[i]
        theirs = plane.block(dx, dy, 0)
        sends[i].wait_recv()
        sends.append(plane.send(out.at[theirs], out.at[theirs], sems, first + 4 + i, (0, 0, 1)))
    for copy in sends[3:]:
        copy.wait_recv()
    for copy in sends:
        copy.wait_send()


def gather_rows(plane, out, sems, first):
    mine = plane.y * 2 + plane.c
    theirs = flip(plane.y, 1) * 2 + plane.c
    over = plane.send(out.at[mine], out.at[mine], sems, first, (0, 1, 0))
    beside = plane.send(out.at[mine], out.at[mine], sems, first + 1, (0, 0, 1))
    over.wait_recv()
    onward = plane.send(out.at[theirs], out.at[theirs], sems, first + 2, (0, 0, 1))
    beside.wait_recv()
    onward.wait_recv()
    for copy in (over, beside, onward):
        copy.wait_send()


def forward_kernel(part, residual, gain, after, normed, from_core, to_chip, from_chip, sems):
    plane = Plane()
    plane.greet(ALL_RELATIONS)
    values = residual[...] + reduce_blocks(plane, part, from_core, to_chip, from_chip, sems)
    after[...] = values
    scale = lax.rsqrt(jnp.mean(values * values, axis=-1, keepdims=True) + EPS)
    normed[plane.block(0, 0, 0)] = rounded(values * scale * gain[...])
    gather_blocks(plane, normed, sems, 7)


def back_values(values, gain, grad):
    scale = lax.rsqrt(jnp.mean(values * values, axis=-1, keepdims=True) + EPS)
    gain_part = jnp.sum(grad * values * scale, axis=0, keepdims=True)
    scaled = grad * gain
    side = scale * scaled - values * (scale * scale * scale) * jnp.mean(
        scaled * values, axis=-1, keepdims=True
    )
    return side, gain_part


def backward_kernel(
    part, values, grad, gain, grad_out, gain_part, grad_all, from_core, to_chip, from_chip, sems
):
    plane = Plane()
    plane.greet(ALL_RELATIONS)
    total = reduce_blocks(plane, part, from_core, to_chip, from_chip, sems)
    side, gain_sum = back_values(values[...], gain[...], total)
    gain_part[...] = gain_sum
    result = grad[...] + side
    grad_out[...] = result
    grad_all[plane.block(0, 0, 0)] = rounded(result)
    gather_blocks(plane, grad_all, sems, 7)


def output_kernel(part, residual, out, from_core, to_chip, from_chip, sems):
    plane = Plane()
    plane.greet(ALL_RELATIONS)
    values = residual[...] + reduce_blocks(plane, part, from_core, to_chip, from_chip, sems)
    out[plane.y * 2 + plane.c] = rounded(values)
    gather_rows(plane, out, sems, 7)


def input_kernel(
    part, values, grad, gain, gains_before, out, gains_sum,
    from_core, to_chip, from_chip, sems, sums, beside,
):
    plane = Plane()
    plane.greet(ALL_RELATIONS)
    total = reduce_blocks(plane, part, from_core, to_chip, from_chip, sems)
    side, gain_sum = back_values(values[...], gain[...], total)
    out[plane.y * 2 + plane.c] = grad[...] + side
    sums[0] = gains_before[...]
    sums[0, 0:1] = gain_sum
    pair = plane.send(sums.at[0], beside.at[0], sems, 10, (0, 0, 1))
    pair.wait_recv()
    sums[1] = sums[0] + beside[0]
    across = plane.send(sums.at[1], beside.at[1], sems, 11, (0, 1, 0))
    gather_rows(plane, out, sems, 7)
    across.wait_recv()
    gains_sum[...] = sums[1] + beside[1]
    pair.wait_send()
    across.wait_send()


def weights_kernel(count, groups, others, *refs):
    keeps, gives, sources = refs[:groups], refs[groups : 2 * groups], refs[2 * groups :][:others]
    outs, received = refs[2 * groups + others :][:groups], refs[3 * groups + others :][:others]
    swap_sems, line_sems = refs[3 * groups + 2 * others :]
    plane = Plane()

    def line(i, side):
        at = flip(plane.x, side)
        return Line(count, lambda block: outs[i].at[block, at], line_sems.at[i, side])

    lines = [[line(i, 0), line(i, 1)] for i in range(groups)]
    here = lines[0][0].z
    plane.greet(((1, 0, 0),), lines[0][0])
    swaps = [
        plane.send(gives[i], outs[i].at[here, plane.x], swap_sems, i, (1, 0, 0))
        for i in range(groups)
    ]
    for i in range(groups):
        outs[i][here, plane.x] = keeps[i][...]
        lines[i][0].start(0)
    swaps += [
        plane.send(sources[i], received[i], swap_sems, groups + i, (1, 0, 0))
        for i in range(others)
    ]
    for i in range(groups):
        swaps[i].wait_recv()
        lines[i][1].start(0)
    for step in range(count - 1):
        for side in (0, 1):
            for i in range(groups):
                lines[i][side].onward(step)
    for copy in swaps[groups:]:
        copy.wait_recv()
    for copy in swaps:
        copy.wait_send()
    for i in range(groups):
        lines[i][0].finish()
        lines[i][1].finish()


def gather_kernel(own, out, sems):
    plane = Plane()
    plane.greet(ALL_RELATIONS)
    out[plane.block(0, 0, 0)] = own[...]
    gather_blocks(plane, out, sems, 0)


def scatter_kernel(part, out, from_core, to_chip, from_chip, sems):
    plane = Plane()
    plane.greet(ALL_RELATIONS)
    out[...] = rounded(reduce_blocks(plane, part, from_core, to_chip, from_chip, sems))


def plane_call(kernel, name, number, outs, rows, columns, copies, reduces, operands, more=()):
    whole = pl.BlockSpec(memory_space=pltpu.VMEM)
    scratch = []
    if reduces:
        scratch = [
            pltpu.VMEM((4, rows, columns), jnp.bfloat16),
            pltpu.VMEM((3, rows, columns), jnp.bfloat16),
            pltpu.VMEM((3, rows, columns), jnp.bfloat16),
        ]
    scratch += [pltpu.SemaphoreType.DMA((2, copies)), *more]
    return pl.pallas_call(
        kernel,
        name=name,
        out_shape=outs,
        in_specs=[whole] * len(operands),
        out_specs=jax.tree.map(lambda _: whole, outs),
        scratch_shapes=scratch,
        compiler_params=pltpu.CompilerParams(
            collective_id=number, has_side_effects=True, vmem_limit_bytes=VMEM_LIMIT
        ),
    )(*operands)


def full(shape, dtype=jnp.float32):
    return jax.ShapeDtypeStruct(shape, dtype)


def forward_step(part, residual, gain):
    rows, columns = residual.shape
    return plane_call(
        forward_kernel, "forward_step", 0,
        (full((rows, columns)), full((8, rows, columns), jnp.bfloat16)),
        rows, columns, 14, True, (part, residual, gain),
    )


def backward_step(part, values, grad, gain):
    rows, columns = values.shape
    return plane_call(
        backward_kernel, "backward_step", 1,
        (full((rows, columns)), full((1, columns)), full((8, rows, columns), jnp.bfloat16)),
        rows, columns, 14, True, (part, values, grad, gain),
    )


def output_step(part, residual):
    rows, columns = residual.shape
    return plane_call(
        output_kernel, "output_step", 2, full((4, rows, columns), jnp.bfloat16),
        rows, columns, 10, True, (part, residual),
    )


def input_step(part, values, grad, gain, gains_before):
    rows, columns = values.shape
    return plane_call(
        input_kernel, "input_step", 3, (full((4, rows, columns)), full((8, columns))),
        rows, columns, 12, True, (part, values, grad, gain, gains_before),
        (pltpu.VMEM((2, 8, columns), jnp.float32), pltpu.VMEM((2, 8, columns), jnp.float32)),
    )


def weights_step(keeps, gives, sources, planes):
    anywhere = pl.BlockSpec(memory_space=pl.ANY)
    whole = pl.BlockSpec(memory_space=pltpu.VMEM)
    outs = [full((planes, 2) + keep.shape, keep.dtype) for keep in keeps]
    outs += [full(source.shape, source.dtype) for source in sources]
    groups, others = len(keeps), len(sources)
    results = pl.pallas_call(
        functools.partial(weights_kernel, planes, groups, others),
        name="weights_step",
        out_shape=outs,
        in_specs=[whole] * (2 * groups) + [anywhere] * others,
        out_specs=[whole] * groups + [anywhere] * others,
        scratch_shapes=[
            pltpu.SemaphoreType.DMA((2, groups + others)),
            pltpu.SemaphoreType.DMA((groups, 2, 2, 2, planes - 1)),
        ],
        compiler_params=pltpu.CompilerParams(
            collective_id=6, has_side_effects=True, vmem_limit_bytes=VMEM_LIMIT
        ),
    )(*keeps, *gives, *sources)
    return results[:groups], results[groups:]


def gather_step(own):
    rows, columns = own.shape
    return plane_call(
        gather_kernel, "gather_step", 4, full((8, rows, columns), own.dtype),
        rows, columns, 7, False, (own,),
    )


def scatter_step(part):
    _, rows, columns = part.shape
    return plane_call(
        scatter_kernel, "scatter_step", 5, full((rows, columns), part.dtype),
        rows, columns, 7, True, (part,),
    )


def split_heads(values):
    return values.reshape(2, values.shape[0] // 2, -1, HD)


def merge_heads(values):
    return values.reshape(2 * values.shape[1], -1)


def masked_scores(queries, key_rows, allowed):
    scores = jnp.einsum(
        "bshe,bkhe->bhsk", queries, key_rows, preferred_element_type=jnp.float32
    ) * HD ** (-0.5)
    return jnp.where(allowed[:, None], scores, -1000000000.0)


def attend(queries, key_rows, value_rows, allowed):
    scores = masked_scores(queries, key_rows, allowed)
    log_total = jax.nn.logsumexp(scores, axis=-1, keepdims=True)
    attn_probs = jnp.exp(scores - log_total)
    mixed = jnp.einsum(
        "bhsk,bkhe->bshe", rounded(attn_probs), value_rows, preferred_element_type=jnp.float32
    )
    return (rounded(merge_heads(mixed)), log_total)


def attend_back(queries, key_rows, value_rows, allowed, log_total, grad_mixed):
    attn_probs = jnp.exp(masked_scores(queries, key_rows, allowed) - log_total)
    grad_probs = jnp.einsum(
        "bshe,bkhe->bhsk", grad_mixed, value_rows, preferred_element_type=jnp.float32
    )
    grad_scores = rounded(
        attn_probs * (grad_probs - jnp.sum(attn_probs * grad_probs, axis=-1, keepdims=True))
    )
    grad_queries = jnp.einsum(
        "bhsk,bkhe->bshe", grad_scores, key_rows, preferred_element_type=jnp.float32
    ) * HD ** (-0.5)
    grad_keys = jnp.einsum(
        "bhsk,bshe->bkhe", grad_scores, queries, preferred_element_type=jnp.float32
    ) * HD ** (-0.5)
    grad_values = jnp.einsum(
        "bhsk,bshe->bkhe", rounded(attn_probs), grad_mixed, preferred_element_type=jnp.float32
    )
    return tuple(rounded(merge_heads(g)) for g in (grad_queries, grad_keys, grad_values))


def gated_gelu(gate_up):
    return jax.nn.gelu(gate_up[0], approximate=True) * gate_up[1]


def dot(pattern, left, right):
    return jnp.einsum(pattern, left, right, preferred_element_type=jnp.float32)


SWAP = ((0, 1), (1, 0))


def ignore(*refs):
    del refs


def after(value, *earlier):
    anywhere = pl.BlockSpec(memory_space=pl.ANY)
    return pl.pallas_call(
        ignore,
        name="after",
        out_shape=jax.ShapeDtypeStruct(value.shape, value.dtype),
        in_specs=[anywhere] * (1 + len(earlier)),
        out_specs=anywhere,
        input_output_aliases={0: 0},
    )(value, *earlier)


def either(own, other, x, join):
    return jnp.where(x == 0, join([own, other]), join([other, own]))


def cut_in(weight, x):
    flat = weight.reshape(-1, weight.shape[-1])
    size = flat.shape[1] // 2
    return [lax.dynamic_slice_in_dim(flat, k * size, size, 1) for k in (x, 1 - x)]


def cut_out(weight, x, columns):
    size = weight.shape[0] // 2
    return [
        lax.dynamic_slice_in_dim(weight, k * size, size, 0).reshape(-1, columns)
        for k in (x, 1 - x)
    ]


def gather_group(swapped):
    return lax.all_gather(swapped, "z", axis=0, tiled=True)


def scatter_group(parts):
    return lax.psum_scatter(parts, "z", scatter_dimension=0, tiled=True)


def home_group(share, x):
    give = lax.dynamic_index_in_dim(share, 1 - x, 0, False)
    return lax.dynamic_index_in_dim(share, x, 0, False), lax.ppermute(give, "x", SWAP)


def home(pair, place, shape, axis, x):
    own, other = (half[place[0] : place[1]].reshape(shape) for half in pair)
    joined = either(own, other, x, functools.partial(jnp.concatenate, axis=axis))
    return joined.astype(jnp.float32)


def places(*sizes):
    ends = [sum(sizes[: k + 1]) for k in range(len(sizes))]
    return [(end - size, end) for end, size in zip(ends, sizes)]


def on_device(
    tokens,
    patches,
    lengths,
    patch_keep,
    norm_gains,
    self_qkv,
    self_out,
    cross_q,
    cross_kv,
    cross_out,
    patch_proj,
    ffn_in,
    ffn_out,
    cotangent,
):
    x = lax.axis_index("x")
    m = lax.axis_index("mp")
    slots, width = tokens.shape[1], tokens.shape[2]
    rows = slots // 4
    depth, patch_depth = cross_q.shape[0], patch_proj.shape[0]
    blocks = width // depth
    heads, units = self_out.shape[0] // 2, ffn_out.shape[0] // 2
    def padded(values):
        flat = values.reshape(-1, 3 * depth)
        return jnp.pad(flat, ((0, 0), (0, 16 * heads - 3 * depth))).reshape(-1, 16, heads)

    def unpadded(values):
        return values.reshape(-1, 16 * heads)[:, : 3 * depth].reshape(-1, 3, depth)

    early = [
        cut_in(patch_proj, x),
        cut_in(self_qkv, x),
        [padded(norm_gains)[0]] * 2,
        cut_in(cross_kv, x),
        cut_in(cross_q, x),
        cut_out(self_out, x, heads),
        cut_out(cross_out, x, heads),
    ]
    third, fourth = cut_in(ffn_in, x), cut_out(ffn_out, x, depth)
    facts = jnp.concatenate([patch_keep, lengths[:, None]], axis=1)
    facts = jnp.pad(facts, ((0, 7), (0, 127)))
    sources = (third[1], tokens[0], patches[0], fourth[1], cotangent[0], facts)
    weights, received = weights_step(
        [pair[0] for pair in early], [pair[1] for pair in early], sources, blocks // 2
    )
    third_other, token_other, patch_other, fourth_other, grad_other, facts_other = received
    patch_w, qkv_w, gains, cross_kv_w, cross_q_w, self_out_w, cross_out_w = weights
    third = either(third[0], third_other, x, jnp.stack)
    fourth = either(fourth[0], fourth_other, x, jnp.stack)
    token_all = either(tokens[0], token_other, x, jnp.concatenate)
    patch_all = either(patches[0], patch_other, x, jnp.concatenate)
    grad_all = either(cotangent[0], grad_other, x, jnp.concatenate)
    third_w = gather_group(third)
    patch_w = patch_w.reshape(-1, heads)
    qkv_w = qkv_w.reshape(blocks, 3, depth, heads)
    cross_kv_w = cross_kv_w.reshape(blocks, 2, depth, heads)
    cross_q_w = cross_q_w.reshape(width, heads)
    self_out_w = self_out_w.reshape(blocks, heads, depth)
    cross_out_w = cross_out_w.reshape(blocks, heads, depth)
    gains = unpadded(gains)
    gains = gains.transpose(1, 0, 2).reshape(3, width).astype(jnp.float32)
    gain_of = [gains[i : i + 1] for i in range(3)]
    facts = either(facts[:1], facts_other[:1], x, jnp.concatenate)
    length_at = patch_keep.shape[1]
    patch_keep, lengths = facts[:, :length_at], facts[:, length_at]

    row_index = lax.broadcasted_iota(jnp.int32, (slots, slots), 0)
    col_index = lax.broadcasted_iota(jnp.int32, (slots, slots), 1)
    self_allowed = (col_index <= row_index)[None] & (col_index[None] < lengths[:, None, None])
    cross_allowed = (patch_keep > 0)[:, None, :]

    own_tokens = lax.dynamic_slice_in_dim(tokens[0], m * rows, rows, 0).astype(jnp.float32)
    own_grad = lax.dynamic_slice_in_dim(cotangent[0], m * rows, rows, 0).astype(jnp.float32)

    values = token_all.astype(jnp.float32)
    normed_self = rounded(
        values
        * lax.rsqrt(jnp.mean(values * values, axis=-1, keepdims=True) + EPS)
        * gain_of[0]
    )

    def to_blocks(partial_value):
        return rounded(partial_value).reshape(8, rows, width)

    def from_blocks(values):
        return values.reshape(8 * rows, width)

    def cut(values):
        return values.reshape(values.shape[0], blocks, depth)

    def stacked(*parts):
        return jnp.concatenate([rounded(part).reshape(blocks, -1, heads) for part in parts], axis=1)

    projected = rounded(dot("sbd,bcdf->csf", cut(normed_self), qkv_w))
    self_parts = [split_heads(projected[i]) for i in range(3)]
    mixed_self, total_self = attend(*self_parts, self_allowed)
    memory_part = rounded(dot("pk,kd->pd", patch_all, patch_w))
    memory_blocks = gather_step(memory_part)
    memory = (
        memory_blocks.reshape(2, 4, memory_part.shape[0], -1)
        .transpose(2, 1, 0, 3)
        .reshape(memory_part.shape[0], -1)
    )
    ffn_in_w = third_w.reshape(blocks, 2, depth, units)

    part = dot("sk,bkd->sbd", mixed_self, self_out_w)
    after_self, normed_cross = forward_step(to_blocks(part), own_tokens, gain_of[1])
    normed_cross = from_blocks(normed_cross)

    key_value = rounded(dot("pbd,bcdf->cpf", cut(memory), cross_kv_w))
    query_heads = split_heads(rounded(dot("sd,df->sf", normed_cross, cross_q_w)))
    fourth_w = gather_group(after(fourth, third_w, normed_cross, key_value))
    cross_keys = split_heads(key_value[0])
    cross_values = split_heads(key_value[1])
    mixed_cross, total_cross = attend(query_heads, cross_keys, cross_values, cross_allowed)
    part = dot("sk,bkd->sbd", mixed_cross, cross_out_w)
    after_cross, normed_ffn = forward_step(to_blocks(part), after_self, gain_of[2])
    ffn_out_w = fourth_w.reshape(blocks, units, depth)
    normed_ffn = from_blocks(normed_ffn)

    gate_up = dot("sbd,bcdf->csf", cut(normed_ffn), ffn_in_w)
    hidden = rounded(gated_gelu(gate_up))
    ffn_out_part = rounded(dot("sf,sbd->bfd", hidden, cut(grad_all)))
    ffn_out_share = scatter_group(after(ffn_out_part, fourth_w))
    output_part = to_blocks(dot("sf,bfd->sbd", hidden, ffn_out_w))

    grad_hidden = dot("sbd,bfd->sf", cut(grad_all), ffn_out_w)
    grad_gate_up = rounded(jax.vjp(gated_gelu, gate_up)[1](grad_hidden)[0])
    ffn_in_part = rounded(dot("sbd,csf->bcdf", cut(normed_ffn), grad_gate_up))
    part = dot("csf,bcdf->sbd", grad_gate_up, ffn_in_w)
    grad_after_cross, gain_ffn, grad_all = backward_step(
        to_blocks(part), after_cross, own_grad, gain_of[2]
    )
    ffn_in_part = ffn_in_part.reshape(blocks, 2 * depth, units)
    ffn_in_share = scatter_group(after(ffn_in_part, ffn_out_share, grad_all))
    grad_all = from_blocks(grad_all)

    cross_out_part = dot("sk,sbd->bkd", mixed_cross, cut(grad_all))
    grad_mixed = split_heads(rounded(dot("sbd,bkd->sk", cut(grad_all), cross_out_w)))
    grad_queries, grad_keys, grad_values = attend_back(
        query_heads, cross_keys, cross_values, cross_allowed, total_cross, grad_mixed
    )
    part = dot("sf,df->sd", grad_queries, cross_q_w)
    grad_after_self, gain_cross, grad_all = backward_step(
        to_blocks(part), after_self, grad_after_cross, gain_of[1]
    )
    grad_all = from_blocks(grad_all)
    grad_key_value = jnp.stack([grad_keys, grad_values])
    second_part = stacked(
        dot("pbd,cpf->bcdf", cut(memory), grad_key_value),
        dot("sbd,sf->bdf", cut(normed_cross), grad_queries),
        cross_out_part,
        dot("sk,sbd->bkd", mixed_self, cut(grad_all)),
    )
    grad_mixed = split_heads(rounded(dot("sbd,bkd->sk", cut(grad_all), self_out_w)))
    grad_projected = jnp.stack(attend_back(*self_parts, self_allowed, total_self, grad_mixed))
    second_share = scatter_group(after(second_part, ffn_in_share, grad_projected))

    part = rounded(dot("cpf,bcdf->pbd", grad_key_value, cross_kv_w))
    part = part.reshape(part.shape[0], 4, 2, -1).transpose(2, 1, 0, 3)
    grad_memory = scatter_step(part.reshape(8, *memory_part.shape))
    part = to_blocks(dot("csf,bcdf->sbd", grad_projected, qkv_w))
    gains_before = jnp.concatenate([jnp.zeros_like(gain_ffn), gain_cross, gain_ffn])
    gains_before = jnp.pad(gains_before, ((0, 5), (0, 0)))
    grad_input, gains_part = input_step(
        part, own_tokens, grad_after_self, gain_of[0], gains_before
    )
    gains_part = gains_part[:3].reshape(3, blocks, depth).transpose(1, 0, 2)
    patch_cut = patch_all.reshape(patch_all.shape[0], blocks, patch_depth)
    first_part = stacked(
        dot("pbk,pd->bkd", patch_cut, grad_memory),
        dot("sbd,csf->bcdf", cut(normed_self), grad_projected),
        padded(gains_part),
    )
    first_part = after(first_part, second_share, grad_input)
    first_share = scatter_group(first_part)
    output = output_step(after(output_part, first_part), after_cross)

    pair = home_group(after(ffn_out_share, first_part), x)
    grad_ffn_out = home(pair, (0, units), (units, depth), 0, x)
    pair = home_group(after(ffn_in_share, first_part), x)
    grad_ffn_in = home(pair, (0, 2 * depth), (2, depth, units), 2, x)
    pair = home_group(after(second_share, first_part), x)
    at_kv, at_q, at_cross, at_self = places(2 * depth, depth, depth, depth)
    grad_cross_kv = home(pair, at_kv, (2, depth, heads), 2, x)
    grad_cross_q = home(pair, at_q, (depth, heads), 1, x)
    grad_cross_out = home(pair, at_cross, (heads, depth), 0, x)
    grad_self_out = home(pair, at_self, (heads, depth), 0, x)
    pair = home_group(first_share, x)
    at_patch, at_qkv, at_gain = places(patch_depth, 3 * depth, 16)
    grad_gains = sum(half[at_gain[0] : at_gain[1]].astype(jnp.float32) for half in pair)
    grad_gains = unpadded(grad_gains)[0]
    grad_patch = home(pair, at_patch, (patch_depth, heads), 1, x)
    grad_self_qkv = home(pair, at_qkv, (3, depth, heads), 2, x)
    return (
        output.reshape(1, slots, width),
        grad_input.reshape(1, slots, width),
        grad_gains,
        grad_self_qkv,
        grad_self_out,
        grad_cross_q,
        grad_cross_kv,
        grad_cross_out,
        grad_patch,
        grad_ffn_in,
        grad_ffn_out,
    )


def solution(mesh):
    batch, parts = mesh.shape["batch"], mesh.shape["mp"]
    planes = Mesh(mesh.devices.reshape(batch // 2, 2, parts), ("z", "x", "mp"))
    b = ("z", "x")
    weights = (
        P(None, b, "mp"),
        P("mp", b),
        P(b, "mp"),
        P(None, b, "mp"),
        P("mp", b),
        P(b, "mp"),
        P(None, b, "mp"),
        P("mp", b),
    )
    row = P(b, None, None)
    return jax.shard_map(
        on_device,
        mesh=planes,
        in_specs=(row, row, P(b), P(b, None), P(None, b)) + weights + (row,),
        out_specs=(row, row, P(None, b)) + weights,
        check_vma=False,
    )
```

```python
import functools

import jax
import jax.numpy as jnp
from jax import lax
from jax.experimental import pallas as pl
from jax.experimental.pallas import tpu as pltpu
from jax.sharding import Mesh
from jax.sharding import PartitionSpec as P

HD = 64
EPS = 1e-06
RELATIVE = ((1, 1), (1, 0), (0, 1), (0, 0))
VMEM_LIMIT = 48 * 2**20


def rounded(values):
    return values.astype(jnp.bfloat16)


def flip(value, by):
    return value + by * (1 - 2 * value)


class Plane:
    def __init__(self):
        self.x = lax.axis_index("x")
        part = lax.axis_index("mp")
        self.y = part // 2
        self.c = part % 2

    def device(self, dx, dy, dc):
        return {"x": flip(self.x, dx), "mp": flip(self.y, dy) * 2 + flip(self.c, dc)}

    def block(self, dx, dy, dc):
        return (flip(self.x, dx) * 2 + flip(self.y, dy)) * 2 + flip(self.c, dc)

    def greet(self, relations, line=None):
        barrier = pltpu.get_barrier_semaphore()
        for relation in relations:
            pl.semaphore_signal(
                barrier, inc=1, device_id=self.device(*relation), device_id_type=pl.DeviceIdType.MESH
            )
        if line is None:
            pl.semaphore_wait(barrier, len(relations))
        else:
            line.greet(barrier)
            pl.semaphore_wait(barrier, len(relations) + line.partners)

    def send(self, src, dst, sems, slot, relation):
        copy = pltpu.make_async_remote_copy(
            src_ref=src,
            dst_ref=dst,
            send_sem=sems.at[0, slot],
            recv_sem=sems.at[1, slot],
            device_id=self.device(*relation),
            device_id_type=pl.DeviceIdType.MESH,
        )
        copy.start()
        return copy


class Line:
    def __init__(self, count, at, sems):
        self.z = lax.axis_index("z")
        self.count, self.at, self.sems = count, at, sems
        self.partners = (self.z > 0).astype(jnp.int32) + (self.z < self.count - 1).astype(jnp.int32)

    def greet(self, barrier):
        for there, step in ((self.z > 0, -1), (self.z < self.count - 1, 1)):

            @pl.when(there)
            def signal(step=step):
                pl.semaphore_signal(
                    barrier,
                    inc=1,
                    device_id={"z": self.z + step},
                    device_id_type=pl.DeviceIdType.MESH,
                )

    def copy(self, block, step, way):
        at = self.at(jnp.clip(block, 0, self.count - 1))
        return pltpu.make_async_remote_copy(
            src_ref=at,
            dst_ref=at,
            send_sem=self.sems.at[0, way, step],
            recv_sem=self.sems.at[1, way, step],
            device_id={"z": jnp.clip(self.z + (1 - 2 * way), 0, self.count - 1)},
            device_id_type=pl.DeviceIdType.MESH,
        )

    def sent(self, step, way):
        block = self.z - step * (1 - 2 * way)
        last = self.count - 1
        goes = (self.z < last) & (block >= 0) if way == 0 else (self.z > 0) & (block <= last)
        return block, goes

    def start(self, step):
        for way in (0, 1):
            block, goes = self.sent(step, way)

            @pl.when(goes)
            def begin(block=block, way=way):
                self.copy(block, step, way).start()

    def arrive(self, step):
        for way in (0, 1):
            block = self.z - (step + 1) * (1 - 2 * way)

            @pl.when((block >= 0) & (block < self.count))
            def wait(block=block, way=way):
                self.copy(block, step, way).wait_recv()

    def onward(self, step):
        self.arrive(step)
        if step + 1 < self.count - 1:
            self.start(step + 1)

    def finish(self):
        for step in range(self.count - 1):
            for way in (0, 1):
                block, goes = self.sent(step, way)

                @pl.when(goes)
                def wait(block=block, way=way, step=step):
                    self.copy(block, step, way).wait_send()


ALL_RELATIONS = ((0, 0, 1), (1, 1, 0), (1, 0, 0), (0, 1, 0))
ROW_RELATIONS = ((0, 0, 1), (0, 1, 0))


def row_blocks(plane, part, rows):
    def at(*relation):
        start = pl.multiple_of(plane.block(*relation) * rows, rows)
        return part.at[:, pl.ds(start, rows)]

    return at


def as_rows(values):
    return jnp.concatenate([values[k] for k in range(values.shape[0])], axis=-1)


def reduce_blocks(plane, at, from_core, to_chip, from_chip, sems):
    pair = [
        plane.send(at(dx, dy, 1), from_core.at[i], sems, i, (0, 0, 1))
        for i, (dx, dy) in enumerate(RELATIVE)
    ]
    across = []
    for i, (dx, dy) in enumerate(RELATIVE):
        pair[i].wait_recv()
        both = at(dx, dy, 0)[...].astype(jnp.float32) + from_core[i].astype(jnp.float32)
        if i < 3:
            to_chip[i] = rounded(both)
            across.append(plane.send(to_chip.at[i], from_chip.at[i], sems, 4 + i, (dx, dy, 0)))
    for i in (2, 1, 0):
        across[i].wait_recv()
        both = both + from_chip[i].astype(jnp.float32)
    for copy in pair + across:
        copy.wait_send()
    return both


def reduce_rows(plane, part, from_core, to_chip, from_chip, sems):
    at = row_blocks(plane, part, from_core.shape[2])
    return as_rows(reduce_blocks(plane, at, from_core, to_chip, from_chip, sems))


def gather_blocks(plane, out, sems, first):
    mine = plane.block(0, 0, 0)
    sends = [
        plane.send(out.at[mine], out.at[mine], sems, first + i, (dx, dy, 0))
        for i, (dx, dy) in enumerate(RELATIVE[:3])
    ]
    sends.append(plane.send(out.at[mine], out.at[mine], sems, first + 3, (0, 0, 1)))
    for i in (2, 1, 0):
        dx, dy = RELATIVE[i]
        theirs = plane.block(dx, dy, 0)
        sends[i].wait_recv()
        sends.append(plane.send(out.at[theirs], out.at[theirs], sems, first + 4 + i, (0, 0, 1)))
    for copy in sends[3:]:
        copy.wait_recv()
    for copy in sends:
        copy.wait_send()


def gather_rows(plane, out, sems, first):
    mine = plane.y * 2 + plane.c
    theirs = flip(plane.y, 1) * 2 + plane.c
    over = plane.send(out.at[mine], out.at[mine], sems, first, (0, 1, 0))
    beside = plane.send(out.at[mine], out.at[mine], sems, first + 1, (0, 0, 1))
    over.wait_recv()
    onward = plane.send(out.at[theirs], out.at[theirs], sems, first + 2, (0, 0, 1))
    beside.wait_recv()
    onward.wait_recv()
    for copy in (over, beside, onward):
        copy.wait_send()


def forward_kernel(part, residual, gain, after, normed, from_core, to_chip, from_chip, sems):
    plane = Plane()
    plane.greet(ALL_RELATIONS)
    values = residual[...] + reduce_rows(plane, part, from_core, to_chip, from_chip, sems)
    after[...] = values
    scale = lax.rsqrt(jnp.mean(values * values, axis=-1, keepdims=True) + EPS)
    normed[plane.block(0, 0, 0)] = rounded(values * scale * gain[...])
    gather_blocks(plane, normed, sems, 7)


def back_values(values, gain, grad):
    scale = lax.rsqrt(jnp.mean(values * values, axis=-1, keepdims=True) + EPS)
    gain_part = jnp.sum(grad * values * scale, axis=0, keepdims=True)
    scaled = grad * gain
    side = scale * scaled - values * (scale * scale * scale) * jnp.mean(
        scaled * values, axis=-1, keepdims=True
    )
    return side, gain_part


def backward_kernel(
    part, values, grad, gain, grad_out, gain_part, grad_all, from_core, to_chip, from_chip, sems
):
    plane = Plane()
    plane.greet(ALL_RELATIONS)
    total = reduce_rows(plane, part, from_core, to_chip, from_chip, sems)
    side, gain_sum = back_values(values[...], gain[...], total)
    gain_part[...] = gain_sum
    result = grad[...] + side
    grad_out[...] = result
    grad_all[plane.block(0, 0, 0)] = rounded(result)
    gather_blocks(plane, grad_all, sems, 7)


def output_kernel(
    part, residual, pieces, out, pieces_sum,
    from_core, to_chip, from_chip, sems, arrived, piece_sems,
):
    plane = Plane()
    z, planes = lax.axis_index("z"), pieces.shape[0]
    others = [lax.rem(z + step, planes) for step in range(1, planes)]
    barrier = pltpu.get_barrier_semaphore()
    for target in [{"z": other} for other in others] + [plane.device(*r) for r in ALL_RELATIONS]:
        pl.semaphore_signal(
            barrier, inc=1, device_id=target, device_id_type=pl.DeviceIdType.MESH
        )
    pl.semaphore_wait(barrier, len(others) + len(ALL_RELATIONS))
    copies = []
    for step, other in enumerate(others):
        copy = pltpu.make_async_remote_copy(
            src_ref=pieces.at[other],
            dst_ref=arrived.at[step],
            send_sem=piece_sems.at[0, step],
            recv_sem=piece_sems.at[1, step],
            device_id={"z": other},
            device_id_type=pl.DeviceIdType.MESH,
        )
        copy.start()
        copies.append(copy)
    values = residual[...] + reduce_rows(plane, part, from_core, to_chip, from_chip, sems)
    out[plane.y * 2 + plane.c] = rounded(values)
    gather_rows(plane, out, sems, 7)
    total = pieces[z].astype(jnp.float32)
    for step, copy in enumerate(copies):
        copy.wait_recv()
        total = total + arrived[step].astype(jnp.float32)
    pieces_sum[...] = total
    for copy in copies:
        copy.wait_send()


def input_kernel(
    part, values, grad, gain, gains_before, out, gains_sum,
    from_core, to_chip, from_chip, sems, sums, beside,
):
    plane = Plane()
    plane.greet(ALL_RELATIONS)
    total = reduce_rows(plane, part, from_core, to_chip, from_chip, sems)
    side, gain_sum = back_values(values[...], gain[...], total)
    out[plane.y * 2 + plane.c] = grad[...] + side
    sums[0] = gains_before[...]
    sums[0, 0:1] = gain_sum
    pair = plane.send(sums.at[0], beside.at[0], sems, 10, (0, 0, 1))
    pair.wait_recv()
    sums[1] = sums[0] + beside[0]
    across = plane.send(sums.at[1], beside.at[1], sems, 11, (0, 1, 0))
    gather_rows(plane, out, sems, 7)
    across.wait_recv()
    gains_sum[...] = sums[1] + beside[1]
    pair.wait_send()
    across.wait_send()


def weights_kernel(count, groups, others, *refs):
    keeps, gives, sources = refs[:groups], refs[groups : 2 * groups], refs[2 * groups :][:others]
    outs, received = refs[2 * groups + others :][:groups], refs[3 * groups + others :][:others]
    swap_sems, line_sems = refs[3 * groups + 2 * others :]
    plane = Plane()

    def line(i, side):
        at = flip(plane.x, side)
        return Line(count, lambda block: outs[i].at[block, at], line_sems.at[i, side])

    lines = [[line(i, 0), line(i, 1)] for i in range(groups)]
    here = lines[0][0].z
    plane.greet(((1, 0, 0),), lines[0][0])
    swaps = [
        plane.send(gives[i], outs[i].at[here, plane.x], swap_sems, i, (1, 0, 0))
        for i in range(groups)
    ]
    for i in range(groups):
        outs[i][here, plane.x] = keeps[i][...]
        lines[i][0].start(0)
    swaps += [
        plane.send(sources[i], received[i], swap_sems, groups + i, (1, 0, 0))
        for i in range(others)
    ]
    for i in range(groups):
        swaps[i].wait_recv()
        lines[i][1].start(0)
    for step in range(count - 1):
        for side in (0, 1):
            for i in range(groups):
                lines[i][side].onward(step)
    for copy in swaps[groups:]:
        copy.wait_recv()
    for copy in swaps:
        copy.wait_send()
    for i in range(groups):
        lines[i][0].finish()
        lines[i][1].finish()


def gather_kernel(own, out, sems):
    plane = Plane()
    plane.greet(ALL_RELATIONS)
    out[plane.block(0, 0, 0)] = own[...]
    gather_blocks(plane, out, sems, 0)


def scatter_kernel(part, out, from_core, to_chip, from_chip, sems):
    plane = Plane()
    plane.greet(ALL_RELATIONS)
    out[...] = rounded(
        reduce_blocks(
            plane, lambda *r: part.at[plane.block(*r)], from_core, to_chip, from_chip, sems
        )
    )


def plane_call(kernel, name, number, outs, block, copies, operands, more=()):
    whole = pl.BlockSpec(memory_space=pltpu.VMEM)
    scratch = [pltpu.VMEM((k,) + block, jnp.bfloat16) for k in (4, 3, 3)] if block else []
    scratch += [pltpu.SemaphoreType.DMA((2, copies)), *more]
    return pl.pallas_call(
        kernel,
        name=name,
        out_shape=outs,
        in_specs=[whole] * len(operands),
        out_specs=jax.tree.map(lambda _: whole, outs),
        scratch_shapes=scratch,
        compiler_params=pltpu.CompilerParams(
            collective_id=number, has_side_effects=True, vmem_limit_bytes=VMEM_LIMIT
        ),
    )(*operands)


def block_of(part, rows):
    return (part.shape[0], rows, part.shape[2])


def full(shape, dtype=jnp.float32):
    return jax.ShapeDtypeStruct(shape, dtype)


def forward_step(part, residual, gain):
    rows, columns = residual.shape
    return plane_call(
        forward_kernel, "forward_step", 0,
        (full((rows, columns)), full((8, rows, columns), jnp.bfloat16)),
        block_of(part, rows), 14, (part, residual, gain),
    )


def backward_step(part, values, grad, gain):
    rows, columns = values.shape
    return plane_call(
        backward_kernel, "backward_step", 1,
        (full((rows, columns)), full((1, columns)), full((8, rows, columns), jnp.bfloat16)),
        block_of(part, rows), 14, (part, values, grad, gain),
    )


def output_step(part, residual, pieces):
    rows, columns = residual.shape
    others, shape = pieces.shape[0] - 1, pieces.shape[1:]
    return plane_call(
        output_kernel, "output_step", 2,
        (full((4, rows, columns), jnp.bfloat16), full(shape)),
        block_of(part, rows), 10, (part, residual, pieces),
        (pltpu.VMEM((others,) + shape, pieces.dtype), pltpu.SemaphoreType.DMA((2, others))),
    )


def input_step(part, values, grad, gain, gains_before):
    rows, columns = values.shape
    return plane_call(
        input_kernel, "input_step", 3, (full((4, rows, columns)), full((8, columns))),
        block_of(part, rows), 12, (part, values, grad, gain, gains_before),
        (pltpu.VMEM((2, 8, columns), jnp.float32), pltpu.VMEM((2, 8, columns), jnp.float32)),
    )


def weights_step(keeps, gives, sources, planes):
    anywhere = pl.BlockSpec(memory_space=pl.ANY)
    whole = pl.BlockSpec(memory_space=pltpu.VMEM)
    outs = [full((planes, 2) + keep.shape, keep.dtype) for keep in keeps]
    outs += [full(source.shape, source.dtype) for source in sources]
    groups, others = len(keeps), len(sources)
    results = pl.pallas_call(
        functools.partial(weights_kernel, planes, groups, others),
        name="weights_step",
        out_shape=outs,
        in_specs=[whole] * (2 * groups) + [anywhere] * others,
        out_specs=[whole] * groups + [anywhere] * others,
        scratch_shapes=[
            pltpu.SemaphoreType.DMA((2, groups + others)),
            pltpu.SemaphoreType.DMA((groups, 2, 2, 2, planes - 1)),
        ],
        compiler_params=pltpu.CompilerParams(
            collective_id=6, has_side_effects=True, vmem_limit_bytes=VMEM_LIMIT
        ),
    )(*keeps, *gives, *sources)
    return results[:groups], results[groups:]


def gather_step(own):
    rows, columns = own.shape
    return plane_call(
        gather_kernel, "gather_step", 4, full((8, rows, columns), own.dtype),
        None, 7, (own,),
    )


def scatter_step(part):
    _, rows, columns = part.shape
    return plane_call(
        scatter_kernel, "scatter_step", 5, full((rows, columns), part.dtype),
        (rows, columns), 7, (part,),
    )


def split_heads(values):
    return values.reshape(2, values.shape[0] // 2, -1, HD)


def merge_heads(values):
    return values.reshape(2 * values.shape[1], -1)


def masked_scores(queries, key_rows, allowed):
    scores = jnp.einsum(
        "bshe,bkhe->bhsk", queries, key_rows, preferred_element_type=jnp.float32
    ) * HD ** (-0.5)
    return jnp.where(allowed[:, None], scores, -1000000000.0)


def attend(queries, key_rows, value_rows, allowed):
    scores = masked_scores(queries, key_rows, allowed)
    log_total = jax.nn.logsumexp(scores, axis=-1, keepdims=True)
    attn_probs = jnp.exp(scores - log_total)
    mixed = jnp.einsum(
        "bhsk,bkhe->bshe", rounded(attn_probs), value_rows, preferred_element_type=jnp.float32
    )
    return (rounded(merge_heads(mixed)), log_total)


def attend_back(queries, key_rows, value_rows, allowed, log_total, grad_mixed):
    attn_probs = jnp.exp(masked_scores(queries, key_rows, allowed) - log_total)
    grad_probs = jnp.einsum(
        "bshe,bkhe->bhsk", grad_mixed, value_rows, preferred_element_type=jnp.float32
    )
    grad_scores = rounded(
        attn_probs * (grad_probs - jnp.sum(attn_probs * grad_probs, axis=-1, keepdims=True))
    )
    grad_queries = jnp.einsum(
        "bhsk,bkhe->bshe", grad_scores, key_rows, preferred_element_type=jnp.float32
    ) * HD ** (-0.5)
    grad_keys = jnp.einsum(
        "bhsk,bshe->bkhe", grad_scores, queries, preferred_element_type=jnp.float32
    ) * HD ** (-0.5)
    grad_values = jnp.einsum(
        "bhsk,bshe->bkhe", rounded(attn_probs), grad_mixed, preferred_element_type=jnp.float32
    )
    return tuple(rounded(merge_heads(g)) for g in (grad_queries, grad_keys, grad_values))


def gated_gelu(gate_up):
    return jax.nn.gelu(gate_up[0], approximate=True) * gate_up[1]


def dot(pattern, left, right):
    return jnp.einsum(pattern, left, right, preferred_element_type=jnp.float32)


SWAP = ((0, 1), (1, 0))


def ignore(*refs):
    del refs


def after(value, *earlier):
    anywhere = pl.BlockSpec(memory_space=pl.ANY)
    return pl.pallas_call(
        ignore,
        name="after",
        out_shape=jax.ShapeDtypeStruct(value.shape, value.dtype),
        in_specs=[anywhere] * (1 + len(earlier)),
        out_specs=anywhere,
        input_output_aliases={0: 0},
    )(value, *earlier)


def either(own, other, x, join):
    return jnp.where(x == 0, join([own, other]), join([other, own]))


def cut_in(weight, x):
    flat = weight.reshape(-1, weight.shape[-1])
    size = flat.shape[1] // 2
    return [lax.dynamic_slice_in_dim(flat, k * size, size, 1) for k in (x, 1 - x)]


def cut_out(weight, x, columns):
    size = weight.shape[0] // 2
    return [
        lax.dynamic_slice_in_dim(weight, k * size, size, 0).reshape(-1, columns)
        for k in (x, 1 - x)
    ]


def gather_group(swapped):
    return lax.all_gather(swapped, "z", axis=0, tiled=True)


def scatter_group(parts):
    return lax.psum_scatter(parts, "z", scatter_dimension=0, tiled=True)


def home_group(share, x):
    give = rounded(lax.dynamic_index_in_dim(share, 1 - x, 0, False))
    return lax.dynamic_index_in_dim(share, x, 0, False), lax.ppermute(give, "x", SWAP)


def home(pair, place, shape, axis, x):
    own, other = (
        half[place[0] : place[1]].reshape(shape).astype(jnp.float32) for half in pair
    )
    return either(own, other, x, functools.partial(jnp.concatenate, axis=axis))


def places(*sizes):
    ends = [sum(sizes[: k + 1]) for k in range(len(sizes))]
    return [(end - size, end) for end, size in zip(ends, sizes)]


def on_device(
    tokens,
    patches,
    lengths,
    patch_keep,
    norm_gains,
    self_qkv,
    self_out,
    cross_q,
    cross_kv,
    cross_out,
    patch_proj,
    ffn_in,
    ffn_out,
    cotangent,
):
    x = lax.axis_index("x")
    m = lax.axis_index("mp")
    slots, width = tokens.shape[1], tokens.shape[2]
    rows = slots // 4
    depth, patch_depth = cross_q.shape[0], patch_proj.shape[0]
    blocks = width // depth
    heads, units = self_out.shape[0] // 2, ffn_out.shape[0] // 2
    def padded(values):
        flat = values.reshape(-1, 3 * depth)
        return jnp.pad(flat, ((0, 0), (0, 16 * heads - 3 * depth))).reshape(-1, 16, heads)

    def unpadded(values):
        return values.reshape(-1, 16 * heads)[:, : 3 * depth].reshape(-1, 3, depth)

    early = [
        cut_in(patch_proj, x),
        cut_in(self_qkv, x),
        [padded(norm_gains)[0]] * 2,
        cut_in(cross_kv, x),
        cut_in(cross_q, x),
        cut_out(self_out, x, heads),
        cut_out(cross_out, x, heads),
    ]
    third, fourth = cut_in(ffn_in, x), cut_out(ffn_out, x, depth)
    facts = jnp.concatenate([patch_keep, lengths[:, None]], axis=1)
    facts = jnp.pad(facts, ((0, 7), (0, 127)))
    sources = (third[1], tokens[0], patches[0], fourth[1], cotangent[0], facts)
    weights, received = weights_step(
        [pair[0] for pair in early], [pair[1] for pair in early], sources, blocks // 2
    )
    third_other, token_other, patch_other, fourth_other, grad_other, facts_other = received
    patch_w, qkv_w, gains, cross_kv_w, cross_q_w, self_out_w, cross_out_w = weights
    third = either(third[0], third_other, x, jnp.stack)
    fourth = either(fourth[0], fourth_other, x, jnp.stack)
    token_all = either(tokens[0], token_other, x, jnp.concatenate)
    patch_all = either(patches[0], patch_other, x, jnp.concatenate)
    grad_all = either(cotangent[0], grad_other, x, jnp.concatenate)
    third_w = gather_group(third)
    patch_w = patch_w.reshape(-1, heads)
    qkv_w = qkv_w.reshape(blocks, 3, depth, heads)
    cross_kv_w = cross_kv_w.reshape(blocks, 2, depth, heads)
    cross_q_w = cross_q_w.reshape(width, heads)
    self_out_w = self_out_w.reshape(blocks, heads, depth)
    cross_out_w = cross_out_w.reshape(blocks, heads, depth)
    gains = unpadded(gains)
    gains = gains.transpose(1, 0, 2).reshape(3, width).astype(jnp.float32)
    gain_of = [gains[i : i + 1] for i in range(3)]
    facts = either(facts[:1], facts_other[:1], x, jnp.concatenate)
    length_at = patch_keep.shape[1]
    patch_keep, lengths = facts[:, :length_at], facts[:, length_at]

    row_index = lax.broadcasted_iota(jnp.int32, (slots, slots), 0)
    col_index = lax.broadcasted_iota(jnp.int32, (slots, slots), 1)
    self_allowed = (col_index <= row_index)[None] & (col_index[None] < lengths[:, None, None])
    cross_allowed = (patch_keep > 0)[:, None, :]

    own_tokens = lax.dynamic_slice_in_dim(tokens[0], m * rows, rows, 0).astype(jnp.float32)
    own_grad = lax.dynamic_slice_in_dim(cotangent[0], m * rows, rows, 0).astype(jnp.float32)

    values = token_all.astype(jnp.float32)
    normed_self = rounded(
        values
        * lax.rsqrt(jnp.mean(values * values, axis=-1, keepdims=True) + EPS)
        * gain_of[0]
    )

    def to_blocks(partial_value):
        partial_value = rounded(partial_value)
        if depth % 128 == 0:
            return partial_value
        return jnp.moveaxis(partial_value, 0, 1).reshape(1, 8 * rows, width)

    def from_blocks(values):
        return values.reshape(8 * rows, width)

    def cut(values):
        return values.reshape(values.shape[0], blocks, depth)

    def stacked(*parts):
        return jnp.concatenate([rounded(part).reshape(blocks, -1, heads) for part in parts], axis=1)

    projected = rounded(dot("sbd,bcdf->csf", cut(normed_self), qkv_w))
    self_parts = [split_heads(projected[i]) for i in range(3)]
    mixed_self, total_self = attend(*self_parts, self_allowed)
    memory_part = rounded(dot("pk,kd->pd", patch_all, patch_w))
    memory_blocks = gather_step(memory_part)
    memory = (
        memory_blocks.reshape(2, 4, memory_part.shape[0], -1)
        .transpose(2, 1, 0, 3)
        .reshape(memory_part.shape[0], -1)
    )
    ffn_in_w = third_w.reshape(blocks, 2, depth, units)

    part = dot("sk,bkd->bsd", mixed_self, self_out_w)
    after_self, normed_cross = forward_step(to_blocks(part), own_tokens, gain_of[1])
    normed_cross = from_blocks(normed_cross)

    key_value = rounded(dot("pbd,bcdf->cpf", cut(memory), cross_kv_w))
    query_heads = split_heads(rounded(dot("sd,df->sf", normed_cross, cross_q_w)))
    cross_keys = split_heads(key_value[0])
    cross_values = split_heads(key_value[1])
    mixed_cross, total_cross = attend(query_heads, cross_keys, cross_values, cross_allowed)
    fourth_w = gather_group(after(fourth, third_w, mixed_cross))
    part = dot("sk,bkd->bsd", mixed_cross, cross_out_w)
    after_cross, normed_ffn = forward_step(to_blocks(part), after_self, gain_of[2])
    normed_ffn = from_blocks(normed_ffn)

    gate_up = dot("sbd,bcdf->csf", cut(normed_ffn), ffn_in_w)
    hidden = rounded(gated_gelu(gate_up))
    ffn_out_w = after(fourth_w, hidden).reshape(blocks, units, depth)
    ffn_out_part = rounded(dot("sf,sbd->bfd", hidden, cut(grad_all)))
    ffn_out_share = scatter_group(after(ffn_out_part, ffn_out_w))
    output_part = to_blocks(dot("sf,bfd->bsd", hidden, ffn_out_w))

    grad_hidden = dot("sbd,bfd->sf", cut(grad_all), ffn_out_w)
    grad_gate_up = rounded(jax.vjp(gated_gelu, gate_up)[1](grad_hidden)[0])
    ffn_in_part = rounded(dot("sbd,csf->bcdf", cut(normed_ffn), grad_gate_up))
    part = dot("csf,bcdf->bsd", grad_gate_up, ffn_in_w)
    grad_after_cross, gain_ffn, grad_all = backward_step(
        to_blocks(part), after_cross, own_grad, gain_of[2]
    )
    ffn_in_part = ffn_in_part.reshape(blocks, 2 * depth, units)
    ffn_in_share = scatter_group(after(ffn_in_part, ffn_out_share, grad_all))
    grad_all = from_blocks(grad_all)

    cross_out_part = dot("sk,sbd->bkd", mixed_cross, cut(grad_all))
    grad_mixed = split_heads(rounded(dot("sbd,bkd->sk", cut(grad_all), cross_out_w)))
    grad_queries, grad_keys, grad_values = attend_back(
        query_heads, cross_keys, cross_values, cross_allowed, total_cross, grad_mixed
    )
    part = dot("sf,bdf->bsd", grad_queries, cross_q_w.reshape(blocks, depth, heads))
    grad_after_self, gain_cross, grad_all = backward_step(
        to_blocks(part), after_self, grad_after_cross, gain_of[1]
    )
    grad_all = from_blocks(grad_all)
    grad_key_value = jnp.stack([grad_keys, grad_values])
    grad_mixed = split_heads(rounded(dot("sbd,bkd->sk", cut(grad_all), self_out_w)))
    grad_projected = jnp.stack(attend_back(*self_parts, self_allowed, total_self, grad_mixed))
    second_part = stacked(
        dot("pbd,cpf->bcdf", cut(memory), grad_key_value),
        dot("sbd,sf->bdf", cut(normed_cross), grad_queries),
        cross_out_part,
        dot("sk,sbd->bkd", mixed_self, cut(grad_all)),
    )
    second_share = scatter_group(after(second_part, ffn_in_share, grad_projected))

    part = rounded(dot("cpf,bcdf->pbd", grad_key_value, cross_kv_w))
    part = part.reshape(part.shape[0], 4, 2, -1).transpose(2, 1, 0, 3)
    grad_memory = scatter_step(part.reshape(8, *memory_part.shape))
    part = to_blocks(dot("csf,bcdf->bsd", grad_projected, qkv_w))
    gains_before = jnp.concatenate([jnp.zeros_like(gain_ffn), gain_cross, gain_ffn])
    gains_before = jnp.pad(gains_before, ((0, 5), (0, 0)))
    grad_input, gains_part = input_step(
        part, own_tokens, grad_after_self, gain_of[0], gains_before
    )
    gains_part = gains_part[:3].reshape(3, blocks, depth).transpose(1, 0, 2)
    patch_cut = patch_all.reshape(patch_all.shape[0], blocks, patch_depth)
    pieces = stacked(dot("pbk,pd->bkd", patch_cut, grad_memory), padded(gains_part))
    pieces = jnp.pad(pieces, ((0, 0), (0, -pieces.shape[1] % 16), (0, 0)))
    pieces = pieces.reshape(blocks // 2, 2, -1, heads)
    output, patch_share = output_step(output_part, after_cross, pieces)
    pair = home_group(after(ffn_out_share, grad_input), x)
    grad_ffn_out = home(pair, (0, units), (units, depth), 0, x)
    pair = home_group(after(ffn_in_share, grad_input), x)
    grad_ffn_in = home(pair, (0, 2 * depth), (2, depth, units), 2, x)
    pair = home_group(patch_share, x)
    at_patch, at_gain = places(patch_depth, 16)
    grad_patch = home(pair, at_patch, (patch_depth, heads), 1, x)
    grad_gains = sum(half[at_gain[0] : at_gain[1]].astype(jnp.float32) for half in pair)
    grad_gains = unpadded(grad_gains)[0]
    first_part = stacked(dot("sbd,csf->bcdf", cut(normed_self), grad_projected))
    first_part = after(first_part, second_share, output)
    first_share = scatter_group(first_part)
    pair = home_group(after(second_share, first_part), x)
    at_kv, at_q, at_cross, at_self = places(2 * depth, depth, depth, depth)
    grad_cross_kv = home(pair, at_kv, (2, depth, heads), 2, x)
    grad_cross_q = home(pair, at_q, (depth, heads), 1, x)
    grad_cross_out = home(pair, at_cross, (heads, depth), 0, x)
    grad_self_out = home(pair, at_self, (heads, depth), 0, x)
    pair = home_group(first_share, x)
    grad_self_qkv = home(pair, (0, 3 * depth), (3, depth, heads), 2, x)
    return (
        output.reshape(1, slots, width),
        grad_input.reshape(1, slots, width),
        grad_gains,
        grad_self_qkv,
        grad_self_out,
        grad_cross_q,
        grad_cross_kv,
        grad_cross_out,
        grad_patch,
        grad_ffn_in,
        grad_ffn_out,
    )


def solution(mesh):
    batch, parts = mesh.shape["batch"], mesh.shape["mp"]
    planes = Mesh(mesh.devices.reshape(batch // 2, 2, parts), ("z", "x", "mp"))
    b = ("z", "x")
    weights = (
        P(None, b, "mp"),
        P("mp", b),
        P(b, "mp"),
        P(None, b, "mp"),
        P("mp", b),
        P(b, "mp"),
        P(None, b, "mp"),
        P("mp", b),
    )
    row = P(b, None, None)
    return jax.shard_map(
        on_device,
        mesh=planes,
        in_specs=(row, row, P(b), P(b, None), P(None, b)) + weights + (row,),
        out_specs=(row, row, P(None, b)) + weights,
        check_vma=False,
    )
```

```python
import functools

import jax
import jax.numpy as jnp
from jax import lax
from jax.experimental import pallas as pl
from jax.experimental.pallas import tpu as pltpu
from jax.sharding import Mesh
from jax.sharding import PartitionSpec as P

HD = 64
EPS = 1e-06
RELATIVE = ((1, 1), (1, 0), (0, 1), (0, 0))
VMEM_LIMIT = 48 * 2**20


def rounded(values):
    return values.astype(jnp.bfloat16)


def flip(value, by):
    return value + by * (1 - 2 * value)


class Plane:
    def __init__(self):
        self.x = lax.axis_index("x")
        part = lax.axis_index("mp")
        self.y = part // 2
        self.c = part % 2

    def device(self, dx, dy, dc):
        return {"x": flip(self.x, dx), "mp": flip(self.y, dy) * 2 + flip(self.c, dc)}

    def block(self, dx, dy, dc):
        return (flip(self.x, dx) * 2 + flip(self.y, dy)) * 2 + flip(self.c, dc)

    def greet(self, relations, line=None):
        barrier = pltpu.get_barrier_semaphore()
        for relation in relations:
            pl.semaphore_signal(
                barrier, inc=1, device_id=self.device(*relation), device_id_type=pl.DeviceIdType.MESH
            )
        if line is None:
            pl.semaphore_wait(barrier, len(relations))
        else:
            line.greet(barrier)
            pl.semaphore_wait(barrier, len(relations) + line.partners)

    def send(self, src, dst, sems, slot, relation):
        copy = pltpu.make_async_remote_copy(
            src_ref=src,
            dst_ref=dst,
            send_sem=sems.at[0, slot],
            recv_sem=sems.at[1, slot],
            device_id=self.device(*relation),
            device_id_type=pl.DeviceIdType.MESH,
        )
        copy.start()
        return copy


class Line:
    def __init__(self, count, at, sems):
        self.z = lax.axis_index("z")
        self.count, self.at, self.sems = count, at, sems
        self.partners = (self.z > 0).astype(jnp.int32) + (self.z < self.count - 1).astype(jnp.int32)

    def greet(self, barrier):
        for there, step in ((self.z > 0, -1), (self.z < self.count - 1, 1)):

            @pl.when(there)
            def signal(step=step):
                pl.semaphore_signal(
                    barrier,
                    inc=1,
                    device_id={"z": self.z + step},
                    device_id_type=pl.DeviceIdType.MESH,
                )

    def copy(self, block, step, way):
        at = self.at(jnp.clip(block, 0, self.count - 1))
        return pltpu.make_async_remote_copy(
            src_ref=at,
            dst_ref=at,
            send_sem=self.sems.at[0, way, step],
            recv_sem=self.sems.at[1, way, step],
            device_id={"z": jnp.clip(self.z + (1 - 2 * way), 0, self.count - 1)},
            device_id_type=pl.DeviceIdType.MESH,
        )

    def sent(self, step, way):
        block = self.z - step * (1 - 2 * way)
        last = self.count - 1
        goes = (self.z < last) & (block >= 0) if way == 0 else (self.z > 0) & (block <= last)
        return block, goes

    def start(self, step):
        for way in (0, 1):
            block, goes = self.sent(step, way)

            @pl.when(goes)
            def begin(block=block, way=way):
                self.copy(block, step, way).start()

    def arrive(self, step):
        for way in (0, 1):
            block = self.z - (step + 1) * (1 - 2 * way)

            @pl.when((block >= 0) & (block < self.count))
            def wait(block=block, way=way):
                self.copy(block, step, way).wait_recv()

    def onward(self, step):
        self.arrive(step)
        if step + 1 < self.count - 1:
            self.start(step + 1)

    def finish(self):
        for step in range(self.count - 1):
            for way in (0, 1):
                block, goes = self.sent(step, way)

                @pl.when(goes)
                def wait(block=block, way=way, step=step):
                    self.copy(block, step, way).wait_send()


ALL_RELATIONS = ((0, 0, 1), (1, 1, 0), (1, 0, 0), (0, 1, 0))
ROW_RELATIONS = ((0, 0, 1), (0, 1, 0))


def row_blocks(plane, part, rows):
    def at(*relation):
        start = pl.multiple_of(plane.block(*relation) * rows, rows)
        return part.at[:, pl.ds(start, rows)]

    return at


def as_rows(values):
    return jnp.concatenate([values[k] for k in range(values.shape[0])], axis=-1)


def reduce_blocks(plane, at, from_core, to_chip, from_chip, sems):
    pair = [
        plane.send(at(dx, dy, 1), from_core.at[i], sems, i, (0, 0, 1))
        for i, (dx, dy) in enumerate(RELATIVE)
    ]
    across = []
    for i, (dx, dy) in enumerate(RELATIVE):
        pair[i].wait_recv()
        both = at(dx, dy, 0)[...].astype(jnp.float32) + from_core[i].astype(jnp.float32)
        if i < 3:
            to_chip[i] = rounded(both)
            across.append(plane.send(to_chip.at[i], from_chip.at[i], sems, 4 + i, (dx, dy, 0)))
    for i in (2, 1, 0):
        across[i].wait_recv()
        both = both + from_chip[i].astype(jnp.float32)
    for copy in pair + across:
        copy.wait_send()
    return both


def reduce_rows(plane, part, from_core, to_chip, from_chip, sems):
    at = row_blocks(plane, part, from_core.shape[2])
    return as_rows(reduce_blocks(plane, at, from_core, to_chip, from_chip, sems))


def gather_blocks(plane, out, sems, first):
    mine = plane.block(0, 0, 0)
    sends = [
        plane.send(out.at[mine], out.at[mine], sems, first + i, (dx, dy, 0))
        for i, (dx, dy) in enumerate(RELATIVE[:3])
    ]
    sends.append(plane.send(out.at[mine], out.at[mine], sems, first + 3, (0, 0, 1)))
    for i in (2, 1, 0):
        dx, dy = RELATIVE[i]
        theirs = plane.block(dx, dy, 0)
        sends[i].wait_recv()
        sends.append(plane.send(out.at[theirs], out.at[theirs], sems, first + 4 + i, (0, 0, 1)))
    for copy in sends[3:]:
        copy.wait_recv()
    for copy in sends:
        copy.wait_send()


def gather_rows(plane, out, sems, first):
    mine = plane.y * 2 + plane.c
    theirs = flip(plane.y, 1) * 2 + plane.c
    over = plane.send(out.at[mine], out.at[mine], sems, first, (0, 1, 0))
    beside = plane.send(out.at[mine], out.at[mine], sems, first + 1, (0, 0, 1))
    over.wait_recv()
    onward = plane.send(out.at[theirs], out.at[theirs], sems, first + 2, (0, 0, 1))
    beside.wait_recv()
    onward.wait_recv()
    for copy in (over, beside, onward):
        copy.wait_send()


def forward_kernel(part, residual, gain, after, normed, from_core, to_chip, from_chip, sems):
    plane = Plane()
    plane.greet(ALL_RELATIONS)
    values = residual[...] + reduce_rows(plane, part, from_core, to_chip, from_chip, sems)
    after[...] = values
    scale = lax.rsqrt(jnp.mean(values * values, axis=-1, keepdims=True) + EPS)
    normed[plane.block(0, 0, 0)] = rounded(values * scale * gain[...])
    gather_blocks(plane, normed, sems, 7)


def back_values(values, gain, grad):
    scale = lax.rsqrt(jnp.mean(values * values, axis=-1, keepdims=True) + EPS)
    gain_part = jnp.sum(grad * values * scale, axis=0, keepdims=True)
    scaled = grad * gain
    side = scale * scaled - values * (scale * scale * scale) * jnp.mean(
        scaled * values, axis=-1, keepdims=True
    )
    return side, gain_part


def backward_kernel(
    part, values, grad, gain, grad_out, gain_part, grad_all, from_core, to_chip, from_chip, sems
):
    plane = Plane()
    plane.greet(ALL_RELATIONS)
    total = reduce_rows(plane, part, from_core, to_chip, from_chip, sems)
    side, gain_sum = back_values(values[...], gain[...], total)
    gain_part[...] = gain_sum
    result = grad[...] + side
    grad_out[...] = result
    grad_all[plane.block(0, 0, 0)] = rounded(result)
    gather_blocks(plane, grad_all, sems, 7)


def output_kernel(
    part, residual, pieces, out, pieces_sum,
    from_core, to_chip, from_chip, sems, arrived, piece_sems,
):
    plane = Plane()
    z, planes = lax.axis_index("z"), pieces.shape[0]
    others = [lax.rem(z + step, planes) for step in range(1, planes)]
    barrier = pltpu.get_barrier_semaphore()
    for target in [{"z": other} for other in others] + [plane.device(*r) for r in ALL_RELATIONS]:
        pl.semaphore_signal(
            barrier, inc=1, device_id=target, device_id_type=pl.DeviceIdType.MESH
        )
    pl.semaphore_wait(barrier, len(others) + len(ALL_RELATIONS))
    copies = []
    for step, other in enumerate(others):
        copy = pltpu.make_async_remote_copy(
            src_ref=pieces.at[other],
            dst_ref=arrived.at[step],
            send_sem=piece_sems.at[0, step],
            recv_sem=piece_sems.at[1, step],
            device_id={"z": other},
            device_id_type=pl.DeviceIdType.MESH,
        )
        copy.start()
        copies.append(copy)
    values = residual[...] + reduce_rows(plane, part, from_core, to_chip, from_chip, sems)
    out[plane.y * 2 + plane.c] = rounded(values)
    gather_rows(plane, out, sems, 7)
    total = pieces[z].astype(jnp.float32)
    for step, copy in enumerate(copies):
        copy.wait_recv()
        total = total + arrived[step].astype(jnp.float32)
    pieces_sum[...] = total
    for copy in copies:
        copy.wait_send()


def input_kernel(
    part, values, grad, gain, gains_before, out, gains_sum,
    from_core, to_chip, from_chip, sems, sums, beside,
):
    plane = Plane()
    plane.greet(ALL_RELATIONS)
    total = reduce_rows(plane, part, from_core, to_chip, from_chip, sems)
    side, gain_sum = back_values(values[...], gain[...], total)
    out[plane.y * 2 + plane.c] = grad[...] + side
    sums[0] = gains_before[...]
    sums[0, 0:1] = gain_sum
    pair = plane.send(sums.at[0], beside.at[0], sems, 10, (0, 0, 1))
    pair.wait_recv()
    sums[1] = sums[0] + beside[0]
    across = plane.send(sums.at[1], beside.at[1], sems, 11, (0, 1, 0))
    gather_rows(plane, out, sems, 7)
    across.wait_recv()
    gains_sum[...] = sums[1] + beside[1]
    pair.wait_send()
    across.wait_send()


def half_of(ref, axis, side):
    if axis is None:
        return ref
    size = ref.shape[axis] // 2
    places = [slice(None)] * len(ref.shape)
    places[axis] = pl.ds(pl.multiple_of(side * size, size), size)
    return ref.at[tuple(places)]


def half_shape(shape, axis):
    return tuple(n // 2 if k == axis else n for k, n in enumerate(shape))


def weights_kernel(count, groups, axes, *refs):
    others = len(axes)
    keeps, gives, sources = refs[:groups], refs[groups : 2 * groups], refs[2 * groups :][:others]
    outs, received = refs[2 * groups + others :][:groups], refs[3 * groups + others :][:others]
    swap_sems, line_sems = refs[3 * groups + 2 * others :]
    plane = Plane()

    def line(i, side):
        at = flip(plane.x, side)
        return Line(count, lambda block: outs[i].at[block, at], line_sems.at[i, side])

    lines = [[line(i, 0), line(i, 1)] for i in range(groups)]
    here = lines[0][0].z
    plane.greet(((1, 0, 0),), lines[0][0])
    swaps = [
        plane.send(gives[i], outs[i].at[here, plane.x], swap_sems, i, (1, 0, 0))
        for i in range(groups)
    ]
    for i in range(groups):
        outs[i][here, plane.x] = keeps[i][...]
        lines[i][0].start(0)
    swaps += [
        plane.send(
            half_of(sources[i], axes[i], 1 - plane.x), received[i], swap_sems, groups + i, (1, 0, 0)
        )
        for i in range(others)
    ]
    for i in range(groups):
        swaps[i].wait_recv()
        lines[i][1].start(0)
    for step in range(count - 1):
        for side in (0, 1):
            for i in range(groups):
                lines[i][side].onward(step)
    for copy in swaps[groups:]:
        copy.wait_recv()
    for copy in swaps:
        copy.wait_send()
    for i in range(groups):
        lines[i][0].finish()
        lines[i][1].finish()


def gather_kernel(own, out, sems):
    plane = Plane()
    plane.greet(ALL_RELATIONS)
    out[plane.block(0, 0, 0)] = own[...]
    gather_blocks(plane, out, sems, 0)


def scatter_kernel(part, out, from_core, to_chip, from_chip, sems):
    plane = Plane()
    plane.greet(ALL_RELATIONS)
    out[...] = rounded(
        reduce_blocks(
            plane, lambda *r: part.at[plane.block(*r)], from_core, to_chip, from_chip, sems
        )
    )


def plane_call(kernel, name, number, outs, block, copies, operands, more=()):
    whole = pl.BlockSpec(memory_space=pltpu.VMEM)
    scratch = [pltpu.VMEM((k,) + block, jnp.bfloat16) for k in (4, 3, 3)] if block else []
    scratch += [pltpu.SemaphoreType.DMA((2, copies)), *more]
    return pl.pallas_call(
        kernel,
        name=name,
        out_shape=outs,
        in_specs=[whole] * len(operands),
        out_specs=jax.tree.map(lambda _: whole, outs),
        scratch_shapes=scratch,
        compiler_params=pltpu.CompilerParams(
            collective_id=number, has_side_effects=True, vmem_limit_bytes=VMEM_LIMIT
        ),
    )(*operands)


def block_of(part, rows):
    return (part.shape[0], rows, part.shape[2])


def full(shape, dtype=jnp.float32):
    return jax.ShapeDtypeStruct(shape, dtype)


def forward_step(part, residual, gain):
    rows, columns = residual.shape
    return plane_call(
        forward_kernel, "forward_step", 0,
        (full((rows, columns)), full((8, rows, columns), jnp.bfloat16)),
        block_of(part, rows), 14, (part, residual, gain),
    )


def backward_step(part, values, grad, gain):
    rows, columns = values.shape
    return plane_call(
        backward_kernel, "backward_step", 1,
        (full((rows, columns)), full((1, columns)), full((8, rows, columns), jnp.bfloat16)),
        block_of(part, rows), 14, (part, values, grad, gain),
    )


def output_step(part, residual, pieces):
    rows, columns = residual.shape
    others, shape = pieces.shape[0] - 1, pieces.shape[1:]
    return plane_call(
        output_kernel, "output_step", 2,
        (full((4, rows, columns), jnp.bfloat16), full(shape)),
        block_of(part, rows), 10, (part, residual, pieces),
        (pltpu.VMEM((others,) + shape, pieces.dtype), pltpu.SemaphoreType.DMA((2, others))),
    )


def input_step(part, values, grad, gain, gains_before):
    rows, columns = values.shape
    return plane_call(
        input_kernel, "input_step", 3, (full((4, rows, columns)), full((8, columns))),
        block_of(part, rows), 12, (part, values, grad, gain, gains_before),
        (pltpu.VMEM((2, 8, columns), jnp.float32), pltpu.VMEM((2, 8, columns), jnp.float32)),
    )


def weights_step(keeps, gives, sources, axes, planes):
    anywhere = pl.BlockSpec(memory_space=pl.ANY)
    whole = pl.BlockSpec(memory_space=pltpu.VMEM)
    outs = [full((planes, 2) + keep.shape, keep.dtype) for keep in keeps]
    outs += [
        full(half_shape(source.shape, axis), source.dtype)
        for source, axis in zip(sources, axes)
    ]
    groups, others = len(keeps), len(sources)
    results = pl.pallas_call(
        functools.partial(weights_kernel, planes, groups, axes),
        name="weights_step",
        out_shape=outs,
        in_specs=[whole] * (2 * groups) + [anywhere] * others,
        out_specs=[whole] * groups + [anywhere] * others,
        scratch_shapes=[
            pltpu.SemaphoreType.DMA((2, groups + others)),
            pltpu.SemaphoreType.DMA((groups, 2, 2, 2, planes - 1)),
        ],
        compiler_params=pltpu.CompilerParams(
            collective_id=6, has_side_effects=True, vmem_limit_bytes=VMEM_LIMIT
        ),
    )(*keeps, *gives, *sources)
    return results[:groups], results[groups:]


def gather_step(own):
    rows, columns = own.shape
    return plane_call(
        gather_kernel, "gather_step", 4, full((8, rows, columns), own.dtype),
        None, 7, (own,),
    )


def scatter_step(part):
    _, rows, columns = part.shape
    return plane_call(
        scatter_kernel, "scatter_step", 5, full((rows, columns), part.dtype),
        (rows, columns), 7, (part,),
    )


def split_heads(values):
    return values.reshape(2, values.shape[0] // 2, -1, HD)


def merge_heads(values):
    return values.reshape(2 * values.shape[1], -1)


def masked_scores(queries, key_rows, allowed):
    scores = jnp.einsum(
        "bshe,bkhe->bhsk", queries, key_rows, preferred_element_type=jnp.float32
    ) * HD ** (-0.5)
    return jnp.where(allowed[:, None], scores, -1000000000.0)


def attend(queries, key_rows, value_rows, allowed):
    scores = masked_scores(queries, key_rows, allowed)
    log_total = jax.nn.logsumexp(scores, axis=-1, keepdims=True)
    attn_probs = jnp.exp(scores - log_total)
    mixed = jnp.einsum(
        "bhsk,bkhe->bshe", rounded(attn_probs), value_rows, preferred_element_type=jnp.float32
    )
    return (rounded(merge_heads(mixed)), log_total)


def attend_back(queries, key_rows, value_rows, allowed, log_total, grad_mixed):
    attn_probs = jnp.exp(masked_scores(queries, key_rows, allowed) - log_total)
    grad_probs = jnp.einsum(
        "bshe,bkhe->bhsk", grad_mixed, value_rows, preferred_element_type=jnp.float32
    )
    grad_scores = rounded(
        attn_probs * (grad_probs - jnp.sum(attn_probs * grad_probs, axis=-1, keepdims=True))
    )
    grad_queries = jnp.einsum(
        "bhsk,bkhe->bshe", grad_scores, key_rows, preferred_element_type=jnp.float32
    ) * HD ** (-0.5)
    grad_keys = jnp.einsum(
        "bhsk,bshe->bkhe", grad_scores, queries, preferred_element_type=jnp.float32
    ) * HD ** (-0.5)
    grad_values = jnp.einsum(
        "bhsk,bshe->bkhe", rounded(attn_probs), grad_mixed, preferred_element_type=jnp.float32
    )
    return tuple(rounded(merge_heads(g)) for g in (grad_queries, grad_keys, grad_values))


def gated_gelu(gate_up):
    return jax.nn.gelu(gate_up[0], approximate=True) * gate_up[1]


def dot(pattern, left, right):
    return jnp.einsum(pattern, left, right, preferred_element_type=jnp.float32)


SWAP = ((0, 1), (1, 0))


def ignore(*refs):
    del refs


def after(value, *earlier):
    anywhere = pl.BlockSpec(memory_space=pl.ANY)
    return pl.pallas_call(
        ignore,
        name="after",
        out_shape=jax.ShapeDtypeStruct(value.shape, value.dtype),
        in_specs=[anywhere] * (1 + len(earlier)),
        out_specs=anywhere,
        input_output_aliases={0: 0},
    )(value, *earlier)


def either(own, other, x, join):
    return jnp.where(x == 0, join([own, other]), join([other, own]))


def cut_in(weight, x):
    flat = weight.reshape(-1, weight.shape[-1])
    size = flat.shape[1] // 2
    return [lax.dynamic_slice_in_dim(flat, k * size, size, 1) for k in (x, 1 - x)]


def cut_out(weight, x, columns):
    size = weight.shape[0] // 2
    return [
        lax.dynamic_slice_in_dim(weight, k * size, size, 0).reshape(-1, columns)
        for k in (x, 1 - x)
    ]


def gather_group(swapped):
    return lax.all_gather(swapped, "z", axis=0, tiled=True)


def scatter_group(parts):
    return lax.psum_scatter(parts, "z", scatter_dimension=0, tiled=True)


def home_group(share, x):
    give = rounded(lax.dynamic_index_in_dim(share, 1 - x, 0, False))
    return lax.dynamic_index_in_dim(share, x, 0, False), lax.ppermute(give, "x", SWAP)


def home(pair, place, shape, axis, x):
    own, other = (
        half[place[0] : place[1]].reshape(shape).astype(jnp.float32) for half in pair
    )
    return either(own, other, x, functools.partial(jnp.concatenate, axis=axis))


def places(*sizes):
    ends = [sum(sizes[: k + 1]) for k in range(len(sizes))]
    return [(end - size, end) for end, size in zip(ends, sizes)]


def on_device(
    tokens,
    patches,
    lengths,
    patch_keep,
    norm_gains,
    self_qkv,
    self_out,
    cross_q,
    cross_kv,
    cross_out,
    patch_proj,
    ffn_in,
    ffn_out,
    cotangent,
):
    x = lax.axis_index("x")
    m = lax.axis_index("mp")
    slots, width = tokens.shape[1], tokens.shape[2]
    rows = slots // 4
    depth, patch_depth = cross_q.shape[0], patch_proj.shape[0]
    blocks = width // depth
    heads, units = self_out.shape[0] // 2, ffn_out.shape[0] // 2
    def padded(values):
        flat = values.reshape(-1, 3 * depth)
        return jnp.pad(flat, ((0, 0), (0, 16 * heads - 3 * depth))).reshape(-1, 16, heads)

    def unpadded(values):
        return values.reshape(-1, 16 * heads)[:, : 3 * depth].reshape(-1, 3, depth)

    early = [
        cut_in(patch_proj, x),
        cut_in(self_qkv, x),
        [padded(norm_gains)[0]] * 2,
        cut_in(cross_kv, x),
        cut_in(cross_q, x),
        cut_out(self_out, x, heads),
        cut_out(cross_out, x, heads),
    ]
    facts = jnp.concatenate([patch_keep, lengths[:, None]], axis=1)
    facts = jnp.pad(facts, ((0, 7), (0, 127)))
    sources = (ffn_in, tokens[0], patches[0], ffn_out, cotangent[0], facts)
    weights, received = weights_step(
        [pair[0] for pair in early], [pair[1] for pair in early],
        sources, (2, None, None, 0, None, None), blocks // 2,
    )
    third_other, token_other, patch_other, fourth_other, grad_other, facts_other = received
    patch_w, qkv_w, gains, cross_kv_w, cross_q_w, self_out_w, cross_out_w = weights
    third = either(cut_in(ffn_in, x)[0], third_other.reshape(-1, units), x, jnp.stack)
    fourth = either(cut_out(ffn_out, x, depth)[0], fourth_other, x, jnp.stack)
    token_all = either(tokens[0], token_other, x, jnp.concatenate)
    patch_all = either(patches[0], patch_other, x, jnp.concatenate)
    grad_all = either(cotangent[0], grad_other, x, jnp.concatenate)
    third_w = gather_group(third)
    patch_w = patch_w.reshape(-1, heads)
    qkv_w = qkv_w.reshape(blocks, 3, depth, heads)
    cross_kv_w = cross_kv_w.reshape(blocks, 2, depth, heads)
    cross_q_w = cross_q_w.reshape(width, heads)
    self_out_w = self_out_w.reshape(blocks, heads, depth)
    cross_out_w = cross_out_w.reshape(blocks, heads, depth)
    gains = unpadded(gains)
    gains = gains.transpose(1, 0, 2).reshape(3, width).astype(jnp.float32)
    gain_of = [gains[i : i + 1] for i in range(3)]
    facts = either(facts[:1], facts_other[:1], x, jnp.concatenate)
    length_at = patch_keep.shape[1]
    patch_keep, lengths = facts[:, :length_at], facts[:, length_at]

    row_index = lax.broadcasted_iota(jnp.int32, (slots, slots), 0)
    col_index = lax.broadcasted_iota(jnp.int32, (slots, slots), 1)
    self_allowed = (col_index <= row_index)[None] & (col_index[None] < lengths[:, None, None])
    cross_allowed = (patch_keep > 0)[:, None, :]

    own_tokens = lax.dynamic_slice_in_dim(tokens[0], m * rows, rows, 0).astype(jnp.float32)
    own_grad = lax.dynamic_slice_in_dim(cotangent[0], m * rows, rows, 0).astype(jnp.float32)

    values = token_all.astype(jnp.float32)
    normed_self = rounded(
        values
        * lax.rsqrt(jnp.mean(values * values, axis=-1, keepdims=True) + EPS)
        * gain_of[0]
    )

    def to_blocks(partial_value):
        partial_value = rounded(partial_value)
        if depth % 128 == 0:
            return partial_value
        return jnp.moveaxis(partial_value, 0, 1).reshape(1, 8 * rows, width)

    def from_blocks(values):
        return values.reshape(8 * rows, width)

    def cut(values):
        return values.reshape(values.shape[0], blocks, depth)

    def stacked(*parts):
        return jnp.concatenate([rounded(part).reshape(blocks, -1, heads) for part in parts], axis=1)

    projected = rounded(dot("sbd,bcdf->csf", cut(normed_self), qkv_w))
    self_parts = [split_heads(projected[i]) for i in range(3)]
    mixed_self, total_self = attend(*self_parts, self_allowed)
    memory_part = rounded(dot("pk,kd->pd", patch_all, patch_w))
    memory_blocks = gather_step(memory_part)
    memory = (
        memory_blocks.reshape(2, 4, memory_part.shape[0], -1)
        .transpose(2, 1, 0, 3)
        .reshape(memory_part.shape[0], -1)
    )
    ffn_in_w = third_w.reshape(blocks, 2, depth, units)

    part = dot("sk,bkd->bsd", mixed_self, self_out_w)
    after_self, normed_cross = forward_step(to_blocks(part), own_tokens, gain_of[1])
    normed_cross = from_blocks(normed_cross)

    key_value = rounded(dot("pbd,bcdf->cpf", cut(memory), cross_kv_w))
    query_heads = split_heads(rounded(dot("sd,df->sf", normed_cross, cross_q_w)))
    cross_keys = split_heads(key_value[0])
    cross_values = split_heads(key_value[1])
    mixed_cross, total_cross = attend(query_heads, cross_keys, cross_values, cross_allowed)
    fourth_w = gather_group(after(fourth, third_w, mixed_cross))
    part = dot("sk,bkd->bsd", mixed_cross, cross_out_w)
    after_cross, normed_ffn = forward_step(to_blocks(part), after_self, gain_of[2])
    normed_ffn = from_blocks(normed_ffn)

    gate_up = dot("sbd,bcdf->csf", cut(normed_ffn), ffn_in_w)
    hidden = rounded(gated_gelu(gate_up))
    ffn_out_w = after(fourth_w, hidden).reshape(blocks, units, depth)
    ffn_out_part = rounded(dot("sf,sbd->bfd", hidden, cut(grad_all)))
    ffn_out_share = scatter_group(after(ffn_out_part, ffn_out_w))
    output_part = to_blocks(dot("sf,bfd->bsd", hidden, ffn_out_w))

    grad_hidden = dot("sbd,bfd->sf", cut(grad_all), ffn_out_w)
    grad_gate_up = rounded(jax.vjp(gated_gelu, gate_up)[1](grad_hidden)[0])
    ffn_in_part = rounded(dot("sbd,csf->bcdf", cut(normed_ffn), grad_gate_up))
    part = dot("csf,bcdf->bsd", grad_gate_up, ffn_in_w)
    grad_after_cross, gain_ffn, grad_all = backward_step(
        to_blocks(part), after_cross, own_grad, gain_of[2]
    )
    ffn_in_part = ffn_in_part.reshape(blocks, 2 * depth, units)
    ffn_in_share = scatter_group(after(ffn_in_part, ffn_out_share, grad_all))
    grad_all = from_blocks(grad_all)

    cross_out_part = dot("sk,sbd->bkd", mixed_cross, cut(grad_all))
    grad_mixed = split_heads(rounded(dot("sbd,bkd->sk", cut(grad_all), cross_out_w)))
    grad_queries, grad_keys, grad_values = attend_back(
        query_heads, cross_keys, cross_values, cross_allowed, total_cross, grad_mixed
    )
    part = dot("sf,bdf->bsd", grad_queries, cross_q_w.reshape(blocks, depth, heads))
    grad_after_self, gain_cross, grad_all = backward_step(
        to_blocks(part), after_self, grad_after_cross, gain_of[1]
    )
    grad_all = from_blocks(grad_all)
    grad_key_value = jnp.stack([grad_keys, grad_values])
    grad_mixed = split_heads(rounded(dot("sbd,bkd->sk", cut(grad_all), self_out_w)))
    grad_projected = jnp.stack(attend_back(*self_parts, self_allowed, total_self, grad_mixed))
    second_part = stacked(
        dot("pbd,cpf->bcdf", cut(memory), grad_key_value),
        dot("sbd,sf->bdf", cut(normed_cross), grad_queries),
        cross_out_part,
        dot("sk,sbd->bkd", mixed_self, cut(grad_all)),
        dot("sbd,csf->bcdf", cut(normed_self), grad_projected[:2]),
    )
    second_share = scatter_group(after(second_part, ffn_in_share, grad_projected))

    part = rounded(dot("cpf,bcdf->pbd", grad_key_value, cross_kv_w))
    part = part.reshape(part.shape[0], 4, 2, -1).transpose(2, 1, 0, 3)
    grad_memory = scatter_step(part.reshape(8, *memory_part.shape))
    part = to_blocks(dot("csf,bcdf->bsd", grad_projected, qkv_w))
    gains_before = jnp.concatenate([jnp.zeros_like(gain_ffn), gain_cross, gain_ffn])
    gains_before = jnp.pad(gains_before, ((0, 5), (0, 0)))
    grad_input, gains_part = input_step(
        part, own_tokens, grad_after_self, gain_of[0], gains_before
    )
    gains_part = gains_part[:3].reshape(3, blocks, depth).transpose(1, 0, 2)
    patch_cut = patch_all.reshape(patch_all.shape[0], blocks, patch_depth)
    pieces = stacked(dot("pbk,pd->bkd", patch_cut, grad_memory), padded(gains_part))
    pieces = jnp.pad(pieces, ((0, 0), (0, -pieces.shape[1] % 16), (0, 0)))
    pieces = pieces.reshape(blocks // 2, 2, -1, heads)
    output, patch_share = output_step(output_part, after_cross, pieces)
    pair = home_group(after(ffn_out_share, grad_input), x)
    grad_ffn_out = home(pair, (0, units), (units, depth), 0, x)
    pair = home_group(after(ffn_in_share, grad_input), x)
    grad_ffn_in = home(pair, (0, 2 * depth), (2, depth, units), 2, x)
    pair = home_group(patch_share, x)
    at_patch, at_gain = places(patch_depth, 16)
    grad_patch = home(pair, at_patch, (patch_depth, heads), 1, x)
    grad_gains = sum(half[at_gain[0] : at_gain[1]].astype(jnp.float32) for half in pair)
    grad_gains = unpadded(grad_gains)[0]
    first_part = stacked(dot("sbd,sf->bdf", cut(normed_self), grad_projected[2]))
    first_part = after(first_part, second_share, output, grad_ffn_out, grad_ffn_in, grad_patch)
    first_share = scatter_group(first_part)
    pair = home_group(after(second_share, first_part), x)
    at_kv, at_q, at_cross, at_self, at_pair = places(
        2 * depth, depth, depth, depth, 2 * depth
    )
    grad_cross_kv = home(pair, at_kv, (2, depth, heads), 2, x)
    grad_cross_q = home(pair, at_q, (depth, heads), 1, x)
    grad_cross_out = home(pair, at_cross, (heads, depth), 0, x)
    grad_self_out = home(pair, at_self, (heads, depth), 0, x)
    grad_pair = home(pair, at_pair, (2, depth, heads), 2, x)
    pair = home_group(first_share, x)
    grad_self_qkv = jnp.concatenate([grad_pair, home(pair, (0, depth), (1, depth, heads), 2, x)])
    return (
        output.reshape(1, slots, width),
        grad_input.reshape(1, slots, width),
        grad_gains,
        grad_self_qkv,
        grad_self_out,
        grad_cross_q,
        grad_cross_kv,
        grad_cross_out,
        grad_patch,
        grad_ffn_in,
        grad_ffn_out,
    )


def solution(mesh):
    batch, parts = mesh.shape["batch"], mesh.shape["mp"]
    planes = Mesh(mesh.devices.reshape(batch // 2, 2, parts), ("z", "x", "mp"))
    b = ("z", "x")
    weights = (
        P(None, b, "mp"),
        P("mp", b),
        P(b, "mp"),
        P(None, b, "mp"),
        P("mp", b),
        P(b, "mp"),
        P(None, b, "mp"),
        P("mp", b),
    )
    row = P(b, None, None)
    return jax.shard_map(
        on_device,
        mesh=planes,
        in_specs=(row, row, P(b), P(b, None), P(None, b)) + weights + (row,),
        out_specs=(row, row, P(None, b)) + weights,
        check_vma=False,
    )
```
